512 devices in a mesh: dp: 16 (over y_hi, x, core), tp: 32 (over z, y_lo).
Axes of the slice: x: 4, y: 8 (y_hi: 2, y_lo: 4; y = y_hi * 4 + y_lo), z: 8, core: 2. Of those that a mesh axis runs over, the one named last changes fastest.
Arguments:
- queries: bfloat16 [512, 128, 576], P(('dp', 'tp')), may hold values from -600 to 600
- latent_cache: bfloat16 [512, 1792, 576], P(('dp', 'tp')), may hold values from -17 to 17
- new_latent: bfloat16 [512, 576], P(('dp', 'tp')), may hold values from -8 to 8
- lengths: int32 [512], P(('dp', 'tp')), may hold values from 112 to 1792, as said below
- order: int32 [512], replicated, may hold values from 0 to 511, each once
- value_up: bfloat16 [128, 512, 128], P('tp'), may hold values from -0.25 to 0.25
- out_proj: bfloat16 [16384, 7168], P('tp', 'dp'), may hold values from -0.046875 to 0.046875
- residual: bfloat16 [512, 7168], P('tp', 'dp'), may hold values from -8 to 8
- norm_gain: bfloat16 [7168], P('dp'), may hold values from 0.099609375 to 1.8984375
- gate_weight: bfloat16 [7168, 18432], P('dp', 'tp'), may hold values from -0.0625 to 0.0625
- up_weight: bfloat16 [7168, 18432], P('dp', 'tp'), may hold values from -0.0625 to 0.0625
- down_weight: bfloat16 [18432, 7168], P('tp', 'dp'), may hold values from -0.046875 to 0.046875
Outputs:
- layer_out: bfloat16 [512, 7168], P('tp', 'dp')
The draws below stay inside these ranges and needn't reach their ends.
Inputs may be any that keep to these rules, and one draw needn't show every extreme that they name: `lengths`: at least 2; some row uses all 1792 positions.
All inputs are finite; a program needn't handle non-finite values.
Results may differ from the reference program's by a relative error of at most 0.013.
Values may be sent and summed in bfloat16 or wider, within the bound.
No kernel may reach another device: no remote copies, remote signals or barrier semaphores. Data moves between devices by JAX's collectives and lax.ppermute only.
A program may use at most 64 MiB of HBM per device.

```python
import jax
import jax.numpy as jnp
from jax import lax

D = 7168
FF = 18432
H = 128
LAT = 512
ROPE = 64
HD = 128
CAP = 1792
ROWS = 512


def draw_latent_cache(key, part):
    key = jax.random.fold_in(key, 7)
    first = jax.random.fold_in(key, 0)
    values = jnp.clip(jax.random.normal(first, (ROWS, CAP, LAT + ROPE), jnp.float32), -6.0, 6.0)
    return values.astype(jnp.bfloat16)


def draw_queries(key, part):
    key = jax.random.fold_in(key, 13)
    first = jax.random.fold_in(key, 0)
    values = jnp.clip(jax.random.normal(first, (ROWS, H, LAT + ROPE), jnp.float32), -6.0, 6.0)
    return values.astype(jnp.bfloat16)


def draw_lengths(key, part):
    key = jax.random.fold_in(key, 5)
    first, second, third = jax.random.split(key, 3)
    lowest = CAP // 16
    powers = jnp.power(2, jax.random.randint(first, (ROWS,), 0, 4)).astype(jnp.int32)
    base = lowest * powers
    extra = jax.random.randint(second, (ROWS,), 0, base)
    lengths = jnp.minimum(base + extra, CAP).astype(jnp.int32)
    chosen = jax.random.randint(third, (), 0, ROWS)
    return lengths.at[chosen].set(CAP).astype(jnp.int32)


def draw_residual(key, part):
    key = jax.random.fold_in(key, 23)
    ramp = jnp.arange(D).astype(jnp.float32) / (D - 1)
    column_scale = 0.2 * jnp.power(10.0, ramp)
    values = jnp.clip(jax.random.normal(key, (ROWS, D), jnp.float32), -4.0, 4.0)
    return (values * column_scale[None, :]).astype(jnp.bfloat16)


def levels(key, dims, cuts, smallest, top_value):
    gain = 1.0
    for axis_at, parts in cuts:
        draws = jax.random.uniform(jax.random.fold_in(jax.random.fold_in(key, 6), axis_at), (parts,), jnp.float32, smallest / len(cuts), top_value / len(cuts))
        gain = gain * jnp.repeat(jnp.exp(draws), dims[axis_at] // parts).reshape((-1,) + (1,) * (len(dims) - 1 - axis_at))
    return gain


def gaussian(key, dims, scale, bound, pieces=(), dtype=jnp.bfloat16):
    array = jax.random.normal(key, dims, jnp.float32) * scale
    if len(pieces) > 0:
        array = levels(key, dims, pieces, -0.22, 0.18) * array
    return jnp.clip(array, min=-bound, max=bound).astype(dtype)


def setup_inputs(seed: int = 0) -> dict:
    arg_keys = jax.random.split(jax.random.key(seed), 13)
    queries = draw_queries(jax.random.fold_in(arg_keys[12], 71), 0)
    latent_cache = draw_latent_cache(jax.random.fold_in(arg_keys[12], 71), 0)
    new_latent = gaussian(arg_keys[2], (ROWS, LAT + ROPE), 2.0, 8.0, ((0, 512),))
    lengths = draw_lengths(jax.random.fold_in(arg_keys[12], 71), 0)
    order = jax.random.permutation(arg_keys[4], ROWS).astype(jnp.int32)
    value_up = gaussian(arg_keys[5], (H, LAT, HD), LAT ** -0.5, 0.25, ((0, 32),))
    out_proj = gaussian(arg_keys[6], (H * HD, D), (H * HD) ** -0.5, 0.046875, ((0, 32), (1, 16)))
    residual = draw_residual(jax.random.fold_in(arg_keys[12], 71), 0)
    norm_gain = jnp.clip(1.0 + 0.18 * jax.random.normal(arg_keys[8], (D,), jnp.float32), 0.099609375, 1.8984375).astype(jnp.bfloat16)
    gate_weight = gaussian(arg_keys[9], (D, FF), D ** -0.5, 0.0625, ((0, 16), (1, 32)))
    up_weight = gaussian(arg_keys[10], (D, FF), D ** -0.5, 0.0625, ((0, 16), (1, 32)))
    down_weight = gaussian(arg_keys[11], (FF, D), FF ** -0.5, 0.046875, ((0, 32), (1, 16)))
    return {"queries": queries, "latent_cache": latent_cache, "new_latent": new_latent, "lengths": lengths, "order": order, "value_up": value_up, "out_proj": out_proj, "residual": residual, "norm_gain": norm_gain, "gate_weight": gate_weight, "up_weight": up_weight, "down_weight": down_weight}


def attend_row(items):
    query, cache, fresh, length = items
    factor = (HD + ROPE) ** (-0.5)
    scores = jnp.dot(query, cache.T, preferred_element_type=jnp.float32) * factor
    places = jnp.arange(CAP)
    scores = jnp.where(places[None, :] < length, scores, -jnp.inf)
    own_score = jnp.dot(query, fresh, preferred_element_type=jnp.float32) * factor
    highest = jnp.maximum(lax.optimization_barrier(jnp.max(scores, axis=1)), own_score)
    expo = jnp.exp(scores - highest[:, None])
    own_expo = jnp.exp(own_score - highest)
    total = lax.optimization_barrier(jnp.sum(expo, axis=1)) + own_expo
    probs = (expo / total[:, None]).astype(jnp.bfloat16)
    own_prob = (own_expo / total).astype(jnp.bfloat16)
    summed = jnp.dot(probs, cache[:, :LAT], preferred_element_type=jnp.float32)
    summed = summed + own_prob.astype(jnp.float32)[:, None] * fresh[:LAT].astype(jnp.float32)[None, :]
    return summed.astype(jnp.bfloat16)

def reference(queries, latent_cache, new_latent, lengths, order, value_up, out_proj, residual, norm_gain, gate_weight, up_weight, down_weight):
    latent_out = lax.map(attend_row, (queries, latent_cache, new_latent, lengths))
    head_values = jnp.einsum('rhl,hlv->rhv', latent_out.astype(jnp.float32), value_up.astype(jnp.float32))
    head_values = head_values.astype(jnp.bfloat16).reshape(ROWS, H * HD)
    attn = jnp.dot(head_values, out_proj, preferred_element_type=jnp.float32)
    mid = (residual.astype(jnp.float32) + attn).astype(jnp.bfloat16)
    mid_wide = mid.astype(jnp.float32)
    meansq = lax.optimization_barrier(jnp.mean(mid_wide * mid_wide, axis=1))
    normed = (mid_wide * lax.rsqrt(meansq + 1e-06)[:, None] * norm_gain.astype(jnp.float32)[None, :]).astype(jnp.bfloat16)
    gate = jnp.dot(normed, gate_weight, preferred_element_type=jnp.float32)
    upper = jnp.dot(normed, up_weight, preferred_element_type=jnp.float32)
    hidden = (jax.nn.silu(gate) * upper).astype(jnp.bfloat16)
    ffn = jnp.dot(hidden, down_weight, preferred_element_type=jnp.float32)
    final = mid_wide + ffn
    return jnp.take(final, order, axis=0).astype(jnp.bfloat16)
```

```python
import jax
import jax.numpy as jnp
from jax import lax
from jax.experimental import pallas as pl
from jax.experimental.pallas import tpu as pltpu
from jax.sharding import PartitionSpec as P

D = 7168
LAT = 512
ROPE = 64
HD = 128
BF = jnp.bfloat16
F32 = jnp.float32


NT = (((1,), (1,)), ((), ()))
VMEM = pl.BlockSpec(memory_space=pltpu.VMEM)
SMEM = pl.BlockSpec(memory_space=pltpu.SMEM)


def call(kernel, out, specs, flops):
    return pl.pallas_call(
        kernel,
        out_shape=out,
        in_specs=specs,
        out_specs=VMEM,
        compiler_params=pltpu.CompilerParams(vmem_limit_bytes=24 * 2**20),
        cost_estimate=pl.CostEstimate(flops=flops, bytes_accessed=2**21, transcendentals=0),
    )


def attn_kernel(first_ref, heads_ref, w1_ref, w2_ref, res_ref, out_ref):
    weights = jnp.concatenate([w1_ref[...], w2_ref[...]], axis=0)
    terms = lax.dot_general(heads_ref[...], weights, NT, preferred_element_type=F32)
    rows, count = heads_ref.shape[0], res_ref.shape[0]
    at_row = lax.broadcasted_iota(jnp.int32, (rows, count), 0)
    at_res = lax.broadcasted_iota(jnp.int32, (rows, count), 1)
    here = jnp.where(at_row == at_res + first_ref[0], 1.0, 0.0).astype(BF)
    terms = terms + jnp.dot(here, res_ref[...], preferred_element_type=F32)
    out_ref[...] = terms.astype(BF)


def ff_kernel(mid_ref, gain_ref, g1_ref, g2_ref, u1_ref, u2_ref, out_ref):
    wide = mid_ref[...].astype(F32)
    squares = jnp.sum(wide * wide, axis=1, keepdims=True)
    high = squares.astype(BF).astype(F32)
    gained = (wide * gain_ref[...].astype(F32)).astype(BF)
    ff = g1_ref.shape[1]
    parts, rows, block = out_ref.shape[0], out_ref.shape[1], out_ref.shape[2] // 2
    for k, (a_ref, b_ref, extra) in enumerate(
        ((g1_ref, g2_ref, high), (u1_ref, u2_ref, squares - high))
    ):
        weights = jnp.concatenate([a_ref[...], b_ref[...]], axis=0)
        term = jnp.dot(gained, weights, preferred_element_type=F32)
        pad = jnp.broadcast_to(extra, (extra.shape[0], block - ff))
        term = jnp.concatenate([term, pad], axis=1)
        for q in range(parts):
            part = term[q * rows : (q + 1) * rows].astype(BF)
            out_ref[q, :, k * block : (k + 1) * block] = part


def down_kernel(order_ref, spots_ref, hidden_ref, w_ref, out_ref):
    pick = jnp.where(order_ref[...] == spots_ref[...], 1.0, 0.0).astype(BF)
    hidden = jnp.dot(pick, hidden_ref[...], preferred_element_type=F32).astype(BF)
    terms = lax.dot_general(hidden, w_ref[...], NT, preferred_element_type=F32)
    out_ref[...] = terms.astype(BF)


def exchange(array, axis, groups):
    return lax.all_to_all(
        array, axis, split_axis=0, concat_axis=0, axis_index_groups=groups, tiled=True
    )


def sum_scatter(terms, axis, count, groups=None):
    return add_blocks(exchange(terms, axis, groups), count)


def add_blocks(got, count):
    got = got.reshape((count, got.shape[0] // count) + got.shape[1:])
    return jnp.sum(got.astype(F32), axis=0)


def gather_rows(rows, axis, count, groups=None):
    copies = jnp.broadcast_to(rows[None], (count,) + rows.shape)
    got = exchange(copies, axis, groups)
    return got.reshape((count * rows.shape[0],) + rows.shape[1:])


def local(
    queries,
    latent_cache,
    new_latent,
    lengths,
    order,
    value_up,
    out_proj,
    residual,
    norm_gain,
    gate_weight,
    up_weight,
    down_weight,
    n_dp,
    n_tp,
):
    core = lax.rem(lax.axis_index("dp"), 2)
    swap = [(i, i ^ 1) for i in range(n_dp)]
    n_x = n_dp // 4
    tp = lax.axis_index("tp")

    def at(y, x, c):
        return (y * n_x + x) * 2 + c

    xs, two = range(n_x), range(2)
    along_x = [[at(y, x, c) for x in xs] for y in two for c in two]
    same_y = [[at(y, x, c) for x in xs for c in two] for y in two]
    across_y = [(i, (i + n_dp // 2) % n_dp) for i in range(n_dp)]
    out_proj2 = lax.ppermute(out_proj, "dp", swap)
    norm_gain2 = lax.ppermute(norm_gain, "dp", swap)
    residual2 = lax.ppermute(residual, "dp", swap)
    factor = (HD + ROPE) ** (-0.5)
    positions = latent_cache.shape[1]
    scores = (
        jnp.einsum("rhc,rpc->rhp", queries, latent_cache, preferred_element_type=jnp.float32)
        * factor
    )
    places = jnp.arange(positions)
    scores = jnp.where(places[None, None, :] < lengths[:, None, None], scores, -jnp.inf)
    own_score = (
        jnp.einsum("rhc,rc->rh", queries, new_latent, preferred_element_type=jnp.float32) * factor
    )
    highest = jnp.maximum(jnp.max(scores, axis=2), own_score)
    expo = jnp.exp(scores - highest[:, :, None])
    own_expo = jnp.exp(own_score - highest)
    total = jnp.sum(expo, axis=2) + own_expo
    probs = (expo / total[:, :, None]).astype(jnp.bfloat16)
    own_prob = (own_expo / total).astype(jnp.bfloat16)
    summed = jnp.einsum(
        "rhp,rpl->rhl", probs, latent_cache[:, :, :LAT], preferred_element_type=jnp.float32
    )
    summed = summed + own_prob.astype(jnp.float32)[:, :, None] * new_latent[:, None, :LAT].astype(
        jnp.float32
    )
    latent_out = summed.astype(jnp.bfloat16)
    both_y = [
        [at(y, x, c) * n_tp + j for y in two for j in range(n_tp)] for x in xs for c in two
    ]
    copies = jnp.broadcast_to(latent_out, (2,) + latent_out.shape[1:])
    copies = copies.reshape((2 * n_tp, -1, LAT))
    owned = exchange(copies, ("dp", "tp"), both_y)
    head_values = jnp.einsum("rhl,hlv->rhv", owned, value_up, preferred_element_type=jnp.float32)
    head_values = head_values.astype(jnp.bfloat16).reshape(owned.shape[0], -1)
    heads_set = gather_rows(head_values, "dp", n_x, along_x)
    places = jnp.arange(n_dp // 2 * n_tp)
    set_dp = (places // n_tp % 2 * n_x + places // (2 * n_tp)) * 2
    set_rows = set_dp * n_tp + places % n_tp
    count = residual.shape[0]
    res_row = tp * count
    res_dp = lax.div(res_row, n_tp)
    res_x, res_y = lax.rem(lax.div(res_dp, 2), n_x), lax.div(res_dp, 2 * n_x)
    first = (res_x * 2 + res_y) * n_tp + lax.rem(res_row, n_tp)
    first = jnp.where(lax.rem(res_dp, 2) == core, first, -count).reshape(1)
    res_pair = jnp.concatenate([residual, residual2], axis=1)
    attn_terms = call(
        attn_kernel,
        jax.ShapeDtypeStruct((heads_set.shape[0], res_pair.shape[1]), BF),
        [SMEM] + [VMEM] * 4,
        2 * heads_set.size * res_pair.shape[1],
    )(first, heads_set, out_proj.T, out_proj2.T, res_pair)
    width = residual.shape[1]
    attn_terms, gate_weight, up_weight = lax.optimization_barrier(
        (attn_terms, gate_weight, up_weight)
    )
    got = exchange(attn_terms, "tp", None)
    gate_weight2 = lax.ppermute(gate_weight, "dp", swap)
    up_weight2 = lax.ppermute(up_weight, "dp", swap)
    got, gate_weight2, up_weight2 = lax.optimization_barrier((got, gate_weight2, up_weight2))
    mid = add_blocks(got, n_tp).astype(BF)
    mid_set = gather_rows(mid, "tp", n_tp)
    mid_here, mid_there = mid_set[:, :width], mid_set[:, width:]
    gain = jnp.concatenate([norm_gain, norm_gain2])[None, :]
    ff = gate_weight.shape[1]
    block = (ff + 127) // 128 * 128
    terms = call(
        ff_kernel,
        jax.ShapeDtypeStruct((n_x, mid_set.shape[0] // n_x, 2 * block), BF),
        [VMEM] * 6,
        4 * mid_set.size * ff,
    )(mid_set, gain, gate_weight, gate_weight2, up_weight, up_weight2)
    terms, mid_there = lax.optimization_barrier((terms, mid_there))
    got = exchange(terms, "dp", along_x).reshape(-1, 2 * block)
    mid_rest = lax.ppermute(mid_there, "dp", swap)
    got, mid_rest = lax.optimization_barrier((got, mid_rest))
    sums = add_blocks(got, n_x)
    sums = sums + lax.ppermute(sums.astype(BF), "dp", across_y).astype(F32)
    meansq = (sums[:, ff] + sums[:, block + ff]) / D
    scale = lax.rsqrt(meansq + 1e-06)[:, None]
    gate = sums[:, :ff] * scale
    upper = sums[:, block : block + ff] * scale
    hidden = (jax.nn.silu(gate) * upper).astype(BF)
    hidden = gather_rows(hidden, "dp", n_x * 2, same_y)
    rows = hidden.shape[0]
    spots = jnp.arange(rows)
    spot_dp = at(spots // n_tp % 2, spots // (4 * n_tp), spots // (2 * n_tp) % 2)
    spot_rows = spot_dp * n_tp + spots % n_tp
    ffn_terms = call(
        down_kernel,
        jax.ShapeDtypeStruct((rows, down_weight.shape[1]), BF),
        [VMEM] * 4,
        2 * rows * ff * (rows + down_weight.shape[1]),
    )(order[:, None], spot_rows[None, :].astype(jnp.int32), hidden, down_weight.T)
    ffn_own = sum_scatter(ffn_terms, "tp", n_tp)
    own_count = ffn_own.shape[0]
    wanted = lax.dynamic_slice_in_dim(order, tp * own_count, own_count)
    pick1 = (wanted[:, None] == (set_rows + core * n_tp)[None, :]).astype(BF)
    pick2 = (wanted[:, None] == (set_rows + (1 - core) * n_tp)[None, :]).astype(BF)
    mid_rows = jnp.dot(pick1, mid_here, preferred_element_type=F32) + jnp.dot(
        pick2, mid_rest, preferred_element_type=F32
    )
    return (mid_rows + ffn_own).astype(BF)


def solution(mesh):
    n_dp, n_tp = mesh.shape["dp"], mesh.shape["tp"]

    def run(*args):
        return local(*args, n_dp=n_dp, n_tp=n_tp)

    placed = (
        P(("dp", "tp"), None, None),
        P(("dp", "tp"), None, None),
        P(("dp", "tp"), None),
        P(("dp", "tp")),
        P(),
        P("tp", None, None),
        P("tp", "dp"),
        P("tp", "dp"),
        P("dp"),
        P("dp", "tp"),
        P("dp", "tp"),
        P("tp", "dp"),
    )
    return jax.shard_map(
        run, mesh=mesh, in_specs=placed, out_specs=P("tp", "dp"), check_vma=False
    )
```

```python
import jax
import jax.numpy as jnp
from jax import lax
from jax.experimental import pallas as pl
from jax.experimental.pallas import tpu as pltpu
from jax.sharding import PartitionSpec as P

D = 7168
LAT = 512
ROPE = 64
HD = 128
BF = jnp.bfloat16
F32 = jnp.float32


NT = (((1,), (1,)), ((), ()))
VMEM = pl.BlockSpec(memory_space=pltpu.VMEM)
SMEM = pl.BlockSpec(memory_space=pltpu.SMEM)


def call(kernel, out, specs, flops):
    return pl.pallas_call(
        kernel,
        out_shape=out,
        in_specs=specs,
        out_specs=VMEM,
        compiler_params=pltpu.CompilerParams(vmem_limit_bytes=24 * 2**20),
        cost_estimate=pl.CostEstimate(flops=flops, bytes_accessed=2**21, transcendentals=0),
    )


def attn_kernel(first_ref, heads_ref, w1_ref, w2_ref, res_ref, out_ref):
    weights = jnp.concatenate([w1_ref[...], w2_ref[...]], axis=0)
    terms = lax.dot_general(heads_ref[...], weights, NT, preferred_element_type=F32)
    rows, count = heads_ref.shape[0], res_ref.shape[0]
    at_row = lax.broadcasted_iota(jnp.int32, (rows, count), 0)
    at_res = lax.broadcasted_iota(jnp.int32, (rows, count), 1)
    here = jnp.where(at_row == at_res + first_ref[0], 1.0, 0.0).astype(BF)
    terms = terms + jnp.dot(here, res_ref[...], preferred_element_type=F32)
    out_ref[...] = terms.astype(BF)


def ff_kernel(mid_ref, gain_ref, g1_ref, g2_ref, u1_ref, u2_ref, out_ref):
    wide = mid_ref[...].astype(F32)
    squares = jnp.sum(wide * wide, axis=1, keepdims=True)
    high = squares.astype(BF).astype(F32)
    gained = (wide * gain_ref[...].astype(F32)).astype(BF)
    ff = g1_ref.shape[1]
    parts, rows, block = out_ref.shape[0], out_ref.shape[1], out_ref.shape[2] // 2
    for k, (a_ref, b_ref, extra) in enumerate(
        ((g1_ref, g2_ref, high), (u1_ref, u2_ref, squares - high))
    ):
        weights = jnp.concatenate([a_ref[...], b_ref[...]], axis=0)
        term = jnp.dot(gained, weights, preferred_element_type=F32)
        pad = jnp.broadcast_to(extra, (extra.shape[0], block - ff))
        term = jnp.concatenate([term, pad], axis=1)
        for q in range(parts):
            part = term[q * rows : (q + 1) * rows].astype(BF)
            out_ref[q, :, k * block : (k + 1) * block] = part


def down_kernel(pick_ref, hidden_ref, w_ref, out_ref):
    half = out_ref.shape[0]
    hidden = hidden_ref[...]
    parts = []
    for k in range(2):
        pick = pick_ref[k * half : (k + 1) * half]
        rows = jnp.dot(pick, hidden, preferred_element_type=F32).astype(BF)
        parts.append(lax.dot_general(rows, w_ref[...], NT, preferred_element_type=F32))
    out_ref[...] = jnp.concatenate(parts, axis=1).astype(BF)


def mid_kernel(got_ref, out_ref):
    total = got_ref[0].astype(F32)
    for k in range(1, got_ref.shape[0]):
        total = total + got_ref[k].astype(F32)
    total = total.astype(BF)
    for k in range(out_ref.shape[0]):
        out_ref[k] = total


def hidden_kernel(mine_ref, theirs_ref, out_ref):
    sums = mine_ref[...] + theirs_ref[...].astype(F32)
    ff, block = out_ref.shape[2], sums.shape[1] // 2
    meansq = (sums[:, ff : ff + 1] + sums[:, block + ff : block + ff + 1]) / D
    scale = lax.rsqrt(meansq + 1e-06)
    gate = sums[:, :ff] * scale
    upper = sums[:, block : block + ff] * scale
    hidden = (gate / (1.0 + jnp.exp(-gate)) * upper).astype(BF)
    for q in range(out_ref.shape[0]):
        out_ref[q] = hidden


def attend_kernel(length_ref, queries_ref, new_ref, cache_ref, out_ref, held, sems):
    positions, piece = cache_ref.shape[1], 512
    copies = []
    for k, start in enumerate(range(0, positions, piece)):
        at = (slice(None), pl.ds(start, min(piece, positions - start)))
        copies.append(pltpu.make_async_copy(cache_ref.at[at], held.at[at], sems.at[k]))
        copies[-1].start()
    factor = (HD + ROPE) ** (-0.5)
    queries = queries_ref[...].T
    new = new_ref[...].astype(F32)
    own = jnp.sum(queries.astype(F32) * new, axis=1, keepdims=True) * factor
    scores, highest = [], own
    for k, start in enumerate(range(0, positions, piece)):
        size = min(piece, positions - start)
        copies[k].wait()
        part = jnp.dot(queries, held[:, start : start + size], preferred_element_type=F32)
        place = lax.broadcasted_iota(jnp.int32, (1, size), 1) + start
        part = jnp.where(place < length_ref[0], part * factor, -jnp.inf)
        scores.append(part)
        highest = jnp.maximum(highest, jnp.max(part, axis=1, keepdims=True))
    total = jnp.exp(own - highest)
    expos = [jnp.exp(part - highest) for part in scores]
    for expo in expos:
        total = total + jnp.sum(expo, axis=1, keepdims=True)
    share = 1.0 / total
    own = (jnp.exp(own - highest) * share).astype(BF).astype(F32)
    probs = jnp.concatenate([(expo * share).astype(BF) for expo in expos], axis=1)
    latent = lax.dot_general(probs, held[:LAT, :], NT, preferred_element_type=F32)
    latent = latent + own * new[:, :LAT]
    count, heads = out_ref.shape[0] // 2, out_ref.shape[1]
    latent = latent.reshape(count, heads, LAT).astype(BF)
    out_ref[:count] = latent
    out_ref[count:] = latent


def exchange(array, axis, groups):
    return lax.all_to_all(
        array, axis, split_axis=0, concat_axis=0, axis_index_groups=groups, tiled=True
    )


def sum_scatter(terms, axis, count, groups=None):
    return add_blocks(exchange(terms, axis, groups), count)


def add_blocks(got, count):
    got = got.reshape((count, got.shape[0] // count) + got.shape[1:])
    return jnp.sum(got.astype(F32), axis=0)


def gather_rows(rows, axis, count, groups=None):
    copies = jnp.broadcast_to(rows[None], (count,) + rows.shape)
    got = exchange(copies, axis, groups)
    return got.reshape((count * rows.shape[0],) + rows.shape[1:])


def local(
    queries,
    latent_cache,
    new_latent,
    lengths,
    order,
    value_up,
    out_proj,
    residual,
    norm_gain,
    gate_weight,
    up_weight,
    down_weight,
    n_dp,
    n_tp,
):
    core = lax.rem(lax.axis_index("dp"), 2)
    swap = [(i, i ^ 1) for i in range(n_dp)]
    n_x = n_dp // 4
    tp = lax.axis_index("tp")

    def at(y, x, c):
        return (y * n_x + x) * 2 + c

    xs, two = range(n_x), range(2)
    along_x = [[at(y, x, c) for x in xs] for y in two for c in two]
    same_y = [[at(y, x, c) for x in xs for c in two] for y in two]
    across_y = [(i, (i + n_dp // 2) % n_dp) for i in range(n_dp)]
    out_proj2 = lax.ppermute(out_proj, "dp", swap)
    norm_gain2 = lax.ppermute(norm_gain, "dp", swap)
    residual2 = lax.ppermute(residual, "dp", swap)
    positions = latent_cache.shape[1]
    copies = pl.pallas_call(
        attend_kernel,
        out_shape=jax.ShapeDtypeStruct((2 * n_tp, queries.shape[1] // n_tp, LAT), BF),
        in_specs=[SMEM, VMEM, VMEM, pl.BlockSpec(memory_space=pl.ANY)],
        out_specs=VMEM,
        scratch_shapes=[
            pltpu.VMEM((LAT + ROPE, positions), BF),
            pltpu.SemaphoreType.DMA(((positions + 511) // 512,)),
        ],
        compiler_params=pltpu.CompilerParams(vmem_limit_bytes=24 * 2**20),
    )(lengths, queries[0].T, new_latent, latent_cache[0].T)
    both_y = [
        [at(y, x, c) * n_tp + j for y in two for j in range(n_tp)] for x in xs for c in two
    ]
    owned = exchange(copies, ("dp", "tp"), both_y)
    head_values = jnp.einsum("rhl,hlv->rhv", owned, value_up, preferred_element_type=jnp.float32)
    head_values = head_values.astype(jnp.bfloat16).reshape(owned.shape[0], -1)
    heads_set = gather_rows(head_values, "dp", n_x, along_x)
    places = jnp.arange(n_dp // 2 * n_tp)
    set_dp = (places // n_tp % 2 * n_x + places // (2 * n_tp)) * 2
    set_rows = set_dp * n_tp + places % n_tp
    count = residual.shape[0]
    res_row = tp * count
    res_dp = lax.div(res_row, n_tp)
    res_x, res_y = lax.rem(lax.div(res_dp, 2), n_x), lax.div(res_dp, 2 * n_x)
    first = (res_x * 2 + res_y) * n_tp + lax.rem(res_row, n_tp)
    first = jnp.where(lax.rem(res_dp, 2) == core, first, -count).reshape(1)
    res_pair = jnp.concatenate([residual, residual2], axis=1)
    attn_terms = call(
        attn_kernel,
        jax.ShapeDtypeStruct((heads_set.shape[0], res_pair.shape[1]), BF),
        [SMEM] + [VMEM] * 4,
        2 * heads_set.size * res_pair.shape[1],
    )(first, heads_set, out_proj.T, out_proj2.T, res_pair)
    width = residual.shape[1]
    attn_terms, gate_weight, up_weight = lax.optimization_barrier(
        (attn_terms, gate_weight, up_weight)
    )
    got = exchange(attn_terms, "tp", None)
    gate_weight2 = lax.ppermute(gate_weight, "dp", swap)
    up_weight2 = lax.ppermute(up_weight, "dp", swap)
    got, gate_weight2, up_weight2 = lax.optimization_barrier((got, gate_weight2, up_weight2))
    got = got.reshape(n_tp, -1, got.shape[1])
    copies = call(mid_kernel, jax.ShapeDtypeStruct(got.shape, BF), [VMEM], got.size)(got)
    mid_set = exchange(copies, "tp", None).reshape(-1, got.shape[2])
    mid_here, mid_there = mid_set[:, :width], mid_set[:, width:]
    gain = jnp.concatenate([norm_gain, norm_gain2])[None, :]
    ff = gate_weight.shape[1]
    block = (ff + 127) // 128 * 128
    terms = call(
        ff_kernel,
        jax.ShapeDtypeStruct((n_x, mid_set.shape[0] // n_x, 2 * block), BF),
        [VMEM] * 6,
        4 * mid_set.size * ff,
    )(mid_set, gain, gate_weight, gate_weight2, up_weight, up_weight2)
    terms, mid_there = lax.optimization_barrier((terms, mid_there))
    got = exchange(terms, "dp", along_x).reshape(-1, 2 * block)
    mid_rest = lax.ppermute(mid_there, "dp", swap)
    got, mid_rest = lax.optimization_barrier((got, mid_rest))
    sums = add_blocks(got, n_x)
    theirs = lax.ppermute(sums.astype(BF), "dp", across_y)
    copies = call(
        hidden_kernel,
        jax.ShapeDtypeStruct((n_x * 2, sums.shape[0], ff), BF),
        [VMEM] * 2,
        8 * sums.size,
    )(sums, theirs)
    copies, order = lax.optimization_barrier((copies, order))
    hidden = exchange(copies, "dp", same_y).reshape(-1, ff)
    rows = hidden.shape[0]
    spots = jnp.arange(rows)
    spot_dp = at(spots // n_tp % 2, spots // (4 * n_tp), spots // (2 * n_tp) % 2)
    spot_rows = spot_dp * n_tp + spots % n_tp
    own_count = rows // n_tp
    listed = order.reshape(n_tp, 2, own_count // 2).swapaxes(0, 1).reshape(rows)
    pick = (listed[:, None] == spot_rows[None, :]).astype(BF)
    hidden, pick = lax.optimization_barrier((hidden, pick))
    width = down_weight.shape[1]
    ffn_terms = call(
        down_kernel,
        jax.ShapeDtypeStruct((rows // 2, 2 * width), BF),
        [VMEM] * 3,
        2 * rows * ff * (rows + width),
    )(pick, hidden, down_weight.T)
    ffn_own = sum_scatter(ffn_terms, "tp", n_tp)
    ffn_own = jnp.concatenate([ffn_own[:, :width], ffn_own[:, width:]], axis=0)
    wanted = lax.dynamic_slice_in_dim(order, tp * own_count, own_count)
    pick1 = (wanted[:, None] == (set_rows + core * n_tp)[None, :]).astype(BF)
    pick2 = (wanted[:, None] == (set_rows + (1 - core) * n_tp)[None, :]).astype(BF)
    mid_rows = jnp.dot(pick1, mid_here, preferred_element_type=F32) + jnp.dot(
        pick2, mid_rest, preferred_element_type=F32
    )
    return (mid_rows + ffn_own).astype(BF)


def solution(mesh):
    n_dp, n_tp = mesh.shape["dp"], mesh.shape["tp"]

    def run(*args):
        return local(*args, n_dp=n_dp, n_tp=n_tp)

    placed = (
        P(("dp", "tp"), None, None),
        P(("dp", "tp"), None, None),
        P(("dp", "tp"), None),
        P(("dp", "tp")),
        P(),
        P("tp", None, None),
        P("tp", "dp"),
        P("tp", "dp"),
        P("dp"),
        P("dp", "tp"),
        P("dp", "tp"),
        P("tp", "dp"),
    )
    return jax.shard_map(
        run, mesh=mesh, in_specs=placed, out_specs=P("tp", "dp"), check_vma=False
    )
```

```python
import jax
import jax.numpy as jnp
from jax import lax
from jax.experimental import pallas as pl
from jax.experimental.pallas import tpu as pltpu
from jax.sharding import PartitionSpec as P

D = 7168
LANES = 128
LAT = 512
ROPE = 64
HD = 128
BF = jnp.bfloat16
F32 = jnp.float32


NT = (((1,), (1,)), ((), ()))
VMEM = pl.BlockSpec(memory_space=pltpu.VMEM)
SMEM = pl.BlockSpec(memory_space=pltpu.SMEM)


def call(kernel, out, specs, flops):
    return pl.pallas_call(
        kernel,
        out_shape=out,
        in_specs=specs,
        out_specs=VMEM,
        compiler_params=pltpu.CompilerParams(vmem_limit_bytes=24 * 2**20),
        cost_estimate=pl.CostEstimate(flops=flops, bytes_accessed=2**21, transcendentals=0),
    )


def attn_kernel(first_ref, heads_ref, w1_ref, w2_ref, res_ref, out_ref):
    weights = jnp.concatenate([w1_ref[...], w2_ref[...]], axis=0)
    terms = lax.dot_general(heads_ref[...], weights, NT, preferred_element_type=F32)
    rows, count = heads_ref.shape[0], res_ref.shape[0]
    at_row = lax.broadcasted_iota(jnp.int32, (rows, count), 0)
    at_res = lax.broadcasted_iota(jnp.int32, (rows, count), 1)
    here = jnp.where(at_row == at_res + first_ref[0], 1.0, 0.0).astype(BF)
    terms = terms + jnp.dot(here, res_ref[...], preferred_element_type=F32)
    out_ref[...] = terms.astype(BF)


def ff_kernel(mid_ref, gain_ref, g1_ref, g2_ref, u1_ref, u2_ref, out_ref):
    wide = mid_ref[...].astype(F32)
    squares = jnp.sum(wide * wide, axis=1, keepdims=True)
    high = squares.astype(BF).astype(F32)
    gained = (wide * gain_ref[...].astype(F32)).astype(BF)
    terms = []
    for a_ref, b_ref in ((g1_ref, g2_ref), (u1_ref, u2_ref)):
        weights = jnp.concatenate([a_ref[...], b_ref[...]], axis=0)
        terms.append(jnp.dot(gained, weights, preferred_element_type=F32))
    terms = jnp.concatenate(terms, axis=1)
    parts, tiles = out_ref.shape[0], terms.shape[1] // LANES
    rows = terms.shape[0] // parts
    for q in range(parts):
        mine = slice(q * rows, (q + 1) * rows)
        pack(out_ref, q, terms[mine], high[mine], (squares - high)[mine])


def pack(out_ref, q, terms, high, low):
    rows, tiles = terms.shape[0], terms.shape[1] // LANES
    for t in range(tiles):
        tile = terms[:, t * LANES : (t + 1) * LANES]
        out_ref[q, t * rows : (t + 1) * rows, :] = tile.astype(BF)
    lane = lax.broadcasted_iota(jnp.int32, (16, LANES), 1)
    extra = jnp.zeros((16, LANES), F32)
    for g in range(rows // 16):
        mine = slice(16 * g, 16 * g + 16)
        extra = jnp.where(lane == 2 * g, high[mine], extra)
        extra = jnp.where(lane == 2 * g + 1, low[mine], extra)
    out_ref[q, tiles * rows : tiles * rows + 16, :] = extra.astype(BF)


def down_kernel(pick_ref, hidden_ref, w_ref, out_ref):
    half = out_ref.shape[0]
    whole, rows = w_ref.shape[1] // LANES, 64
    blocks = []
    for q in range(hidden_ref.shape[0]):
        tiles = [hidden_ref[q, t * rows : (t + 1) * rows, :] for t in range(whole)]
        rest = hidden_ref[q, whole * rows :, :]
        rest = jnp.concatenate([rest[:, : LANES // 2], rest[:, LANES // 2 :]], axis=0)
        blocks.append(jnp.concatenate(tiles + [rest], axis=1))
    hidden = jnp.concatenate(blocks, axis=0)
    parts = []
    for k in range(2):
        pick = pick_ref[k * half : (k + 1) * half]
        rows = jnp.dot(pick, hidden, preferred_element_type=F32).astype(BF)
        parts.append(lax.dot_general(rows, w_ref[...], NT, preferred_element_type=F32))
    out_ref[...] = jnp.concatenate(parts, axis=1).astype(BF)


def mid_kernel(got_ref, out_ref):
    total = got_ref[0].astype(F32)
    for k in range(1, got_ref.shape[0]):
        total = total + got_ref[k].astype(F32)
    total = total.astype(BF)
    for k in range(out_ref.shape[0]):
        out_ref[k] = total


def hidden_kernel(mine_ref, theirs_ref, out_ref):
    sums = mine_ref[...] + theirs_ref[...].astype(F32)
    tiles = sums.shape[0] // 64
    rows = 64
    extra = sums[tiles * rows :]
    squares = jnp.concatenate(
        [
            extra[:, 2 * g : 2 * g + 1] + extra[:, 2 * g + 1 : 2 * g + 2]
            for g in range(rows // 16)
        ],
        axis=0,
    )
    scale = lax.rsqrt(squares / D + 1e-06)
    both = jnp.concatenate([sums[t * rows : (t + 1) * rows] for t in range(tiles)], axis=1)
    ff = both.shape[1] // 2
    gate = both[:, :ff] * scale
    upper = both[:, ff:] * scale
    hidden = (gate / (1.0 + jnp.exp(-gate)) * upper).astype(BF)
    whole = ff // LANES
    rest = hidden[:, whole * LANES :]
    rest = jnp.concatenate([rest[: rows // 2], rest[rows // 2 :]], axis=1)
    for q in range(out_ref.shape[0]):
        for t in range(whole):
            tile = hidden[:, t * LANES : (t + 1) * LANES]
            out_ref[q, t * rows : (t + 1) * rows, :] = tile
        out_ref[q, whole * rows :, :] = rest


def attend_kernel(length_ref, queries_hbm, new_hbm, cache_hbm, out_ref, *scratch):
    held, queries_ref, new_ref, sems = scratch
    positions, piece = held.shape[1], 512
    first = pltpu.make_async_copy(queries_hbm, queries_ref, sems.at[0])
    second = pltpu.make_async_copy(new_hbm, new_ref, sems.at[1])
    first.start()
    second.start()
    copies = []
    for k, start in enumerate(range(0, positions, piece)):
        at = (slice(None), pl.ds(start, min(piece, positions - start)))
        copies.append(pltpu.make_async_copy(cache_hbm.at[at], held.at[at], sems.at[k + 2]))
        copies[-1].start()
    first.wait()
    second.wait()
    factor = (HD + ROPE) ** (-0.5)
    queries = queries_ref[...].T
    new = new_ref[...].astype(F32)
    own = jnp.sum(queries.astype(F32) * new, axis=1, keepdims=True) * factor
    scores, highest = [], own
    for k, start in enumerate(range(0, positions, piece)):
        size = min(piece, positions - start)
        copies[k].wait()
        part = jnp.dot(queries, held[:, start : start + size], preferred_element_type=F32)
        place = lax.broadcasted_iota(jnp.int32, (1, size), 1) + start
        part = jnp.where(place < length_ref[0], part * factor, -jnp.inf)
        scores.append(part)
        highest = jnp.maximum(highest, jnp.max(part, axis=1, keepdims=True))
    total = jnp.exp(own - highest)
    expos = [jnp.exp(part - highest) for part in scores]
    for expo in expos:
        total = total + jnp.sum(expo, axis=1, keepdims=True)
    share = 1.0 / total
    own = (jnp.exp(own - highest) * share).astype(BF).astype(F32)
    probs = jnp.concatenate([(expo * share).astype(BF) for expo in expos], axis=1)
    latent = lax.dot_general(probs, held[:LAT, :], NT, preferred_element_type=F32)
    latent = latent + own * new[:, :LAT]
    count, heads = out_ref.shape[0] // 2, out_ref.shape[1]
    latent = latent.reshape(count, heads, LAT).astype(BF)
    out_ref[:count] = latent
    out_ref[count:] = latent


def exchange(array, axis, groups):
    return lax.all_to_all(
        array, axis, split_axis=0, concat_axis=0, axis_index_groups=groups, tiled=True
    )


def sum_scatter(terms, axis, count, groups=None):
    return add_blocks(exchange(terms, axis, groups), count)


def add_blocks(got, count):
    got = got.reshape((count, got.shape[0] // count) + got.shape[1:])
    return jnp.sum(got.astype(F32), axis=0)


def gather_rows(rows, axis, count, groups=None):
    copies = jnp.broadcast_to(rows[None], (count,) + rows.shape)
    got = exchange(copies, axis, groups)
    return got.reshape((count * rows.shape[0],) + rows.shape[1:])


def local(
    queries,
    latent_cache,
    new_latent,
    lengths,
    order,
    value_up,
    out_proj,
    residual,
    norm_gain,
    gate_weight,
    up_weight,
    down_weight,
    n_dp,
    n_tp,
):
    core = lax.rem(lax.axis_index("dp"), 2)
    swap = [(i, i ^ 1) for i in range(n_dp)]
    n_x = n_dp // 4
    tp = lax.axis_index("tp")

    def at(y, x, c):
        return (y * n_x + x) * 2 + c

    xs, two = range(n_x), range(2)
    along_x = [[at(y, x, c) for x in xs] for y in two for c in two]
    same_y = [[at(y, x, c) for x in xs for c in two] for y in two]
    across_y = [(i, (i + n_dp // 2) % n_dp) for i in range(n_dp)]
    out_proj2 = lax.ppermute(out_proj, "dp", swap)
    norm_gain2 = lax.ppermute(norm_gain, "dp", swap)
    residual2 = lax.ppermute(residual, "dp", swap)
    positions = latent_cache.shape[1]
    copies = pl.pallas_call(
        attend_kernel,
        out_shape=jax.ShapeDtypeStruct((2 * n_tp, queries.shape[1] // n_tp, LAT), BF),
        in_specs=[SMEM] + [pl.BlockSpec(memory_space=pltpu.HBM)] * 3,
        out_specs=VMEM,
        scratch_shapes=[
            pltpu.VMEM((LAT + ROPE, positions), BF),
            pltpu.VMEM((LAT + ROPE, queries.shape[1]), BF),
            pltpu.VMEM((1, LAT + ROPE), BF),
            pltpu.SemaphoreType.DMA(((positions + 511) // 512 + 2,)),
        ],
        compiler_params=pltpu.CompilerParams(vmem_limit_bytes=63 * 2**20 + 15 * 2**16),
    )(lengths, queries[0].T, new_latent, latent_cache[0].T)
    both_y = [
        [at(y, x, c) * n_tp + j for y in two for j in range(n_tp)] for x in xs for c in two
    ]
    owned = exchange(copies, ("dp", "tp"), both_y)
    head_values = jnp.einsum("rhl,hlv->rhv", owned, value_up, preferred_element_type=jnp.float32)
    head_values = head_values.astype(jnp.bfloat16).reshape(owned.shape[0], -1)
    heads_set = gather_rows(head_values, "dp", n_x, along_x)
    places = jnp.arange(n_dp // 2 * n_tp)
    set_dp = (places // n_tp % 2 * n_x + places // (2 * n_tp)) * 2
    set_rows = set_dp * n_tp + places % n_tp
    count = residual.shape[0]
    res_row = tp * count
    res_dp = lax.div(res_row, n_tp)
    res_x, res_y = lax.rem(lax.div(res_dp, 2), n_x), lax.div(res_dp, 2 * n_x)
    first = (res_x * 2 + res_y) * n_tp + lax.rem(res_row, n_tp)
    first = jnp.where(lax.rem(res_dp, 2) == core, first, -count).reshape(1)
    res_pair = jnp.concatenate([residual, residual2], axis=1)
    attn_terms = call(
        attn_kernel,
        jax.ShapeDtypeStruct((heads_set.shape[0], res_pair.shape[1]), BF),
        [SMEM] + [VMEM] * 4,
        2 * heads_set.size * res_pair.shape[1],
    )(first, heads_set, out_proj.T, out_proj2.T, res_pair)
    width = residual.shape[1]
    attn_terms, gate_weight, up_weight = lax.optimization_barrier(
        (attn_terms, gate_weight, up_weight)
    )
    got = exchange(attn_terms, "tp", None)
    gate_weight2 = lax.ppermute(gate_weight, "dp", swap)
    up_weight2 = lax.ppermute(up_weight, "dp", swap)
    got, gate_weight2, up_weight2 = lax.optimization_barrier((got, gate_weight2, up_weight2))
    got = got.reshape(n_tp, -1, got.shape[1])
    copies = call(mid_kernel, jax.ShapeDtypeStruct(got.shape, BF), [VMEM], got.size)(got)
    mid_set = exchange(copies, "tp", None).reshape(-1, got.shape[2])
    mid_here, mid_there = mid_set[:, :width], mid_set[:, width:]
    gain = jnp.concatenate([norm_gain, norm_gain2])[None, :]
    ff = gate_weight.shape[1]
    tall = mid_set.shape[0] // n_x * (2 * ff // LANES) + 16
    terms = call(
        ff_kernel,
        jax.ShapeDtypeStruct((n_x, tall, LANES), BF),
        [VMEM] * 6,
        4 * mid_set.size * ff,
    )(mid_set, gain, gate_weight, gate_weight2, up_weight, up_weight2)
    terms, mid_there = lax.optimization_barrier((terms, mid_there))
    got = exchange(terms, "dp", along_x).reshape(-1, LANES)
    mid_rest = lax.ppermute(mid_there, "dp", swap)
    got, mid_rest = lax.optimization_barrier((got, mid_rest))
    sums = add_blocks(got, n_x)
    theirs = lax.ppermute(sums.astype(BF), "dp", across_y)
    copies = call(
        hidden_kernel,
        jax.ShapeDtypeStruct((n_x * 2, 2 * n_tp * ff // LANES, LANES), BF),
        [VMEM] * 2,
        8 * sums.size,
    )(sums, theirs)
    copies, order = lax.optimization_barrier((copies, order))
    hidden = exchange(copies, "dp", same_y)
    rows = n_dp * n_tp
    spots = jnp.arange(rows)
    spot_dp = at(spots // n_tp % 2, spots // (4 * n_tp), spots // (2 * n_tp) % 2)
    spot_rows = spot_dp * n_tp + spots % n_tp
    own_count = rows // n_tp
    listed = order.reshape(n_tp, 2, own_count // 2).swapaxes(0, 1).reshape(rows)
    pick = (listed[:, None] == spot_rows[None, :]).astype(BF)
    hidden, pick = lax.optimization_barrier((hidden, pick))
    width = down_weight.shape[1]
    ffn_terms = call(
        down_kernel,
        jax.ShapeDtypeStruct((rows // 2, 2 * width), BF),
        [VMEM] * 3,
        2 * rows * ff * (rows + width),
    )(pick, hidden, down_weight.T)
    ffn_own = sum_scatter(ffn_terms, "tp", n_tp)
    ffn_own = jnp.concatenate([ffn_own[:, :width], ffn_own[:, width:]], axis=0)
    wanted = lax.dynamic_slice_in_dim(order, tp * own_count, own_count)
    pick1 = (wanted[:, None] == (set_rows + core * n_tp)[None, :]).astype(BF)
    pick2 = (wanted[:, None] == (set_rows + (1 - core) * n_tp)[None, :]).astype(BF)
    mid_rows = jnp.dot(pick1, mid_here, preferred_element_type=F32) + jnp.dot(
        pick2, mid_rest, preferred_element_type=F32
    )
    return (mid_rows + ffn_own).astype(BF)


def solution(mesh):
    n_dp, n_tp = mesh.shape["dp"], mesh.shape["tp"]

    def run(*args):
        return local(*args, n_dp=n_dp, n_tp=n_tp)

    placed = (
        P(("dp", "tp"), None, None),
        P(("dp", "tp"), None, None),
        P(("dp", "tp"), None),
        P(("dp", "tp")),
        P(),
        P("tp", None, None),
        P("tp", "dp"),
        P("tp", "dp"),
        P("dp"),
        P("dp", "tp"),
        P("dp", "tp"),
        P("tp", "dp"),
    )
    return jax.shard_map(
        run, mesh=mesh, in_specs=placed, out_specs=P("tp", "dp"), check_vma=False
    )
```

```python
import jax
import jax.numpy as jnp
from jax import lax
from jax.experimental import pallas as pl
from jax.experimental.pallas import tpu as pltpu
from jax.sharding import PartitionSpec as P

D = 7168
LANES = 128
LAT = 512
ROPE = 64
HD = 128
BF = jnp.bfloat16
F32 = jnp.float32


NT = (((1,), (1,)), ((), ()))
VMEM = pl.BlockSpec(memory_space=pltpu.VMEM)
SMEM = pl.BlockSpec(memory_space=pltpu.SMEM)


def call(kernel, out, specs, flops):
    return pl.pallas_call(
        kernel,
        out_shape=out,
        in_specs=specs,
        out_specs=VMEM,
        compiler_params=pltpu.CompilerParams(vmem_limit_bytes=24 * 2**20),
        cost_estimate=pl.CostEstimate(flops=flops, bytes_accessed=2**21, transcendentals=0),
    )


def value_kernel(owned_ref, w_ref, out_ref):
    rows, heads, lat = owned_ref.shape
    size = w_ref.shape[1] // heads
    owned = owned_ref[...].reshape(rows * heads, lat)
    full = jnp.dot(owned, w_ref[...], preferred_element_type=F32)
    shape = (rows * heads, heads * size)
    head = lax.rem(lax.broadcasted_iota(jnp.int32, shape, 0), heads)
    block = lax.div(lax.broadcasted_iota(jnp.int32, shape, 1), size)
    full = jnp.where(head == block, full, 0.0).astype(BF)
    at_row = lax.broadcasted_iota(jnp.int32, (rows, rows * heads), 0)
    source = lax.div(lax.broadcasted_iota(jnp.int32, (rows, rows * heads), 1), heads)
    join = jnp.where(at_row == source, 1.0, 0.0).astype(BF)
    values = jnp.dot(join, full, preferred_element_type=F32).astype(BF)
    for q in range(out_ref.shape[0]):
        out_ref[q] = values


def attn_kernel(first_ref, heads_ref, w1_ref, w2_ref, res_ref, out_ref):
    weights = jnp.concatenate([w1_ref[...], w2_ref[...]], axis=0)
    terms = lax.dot_general(heads_ref[...], weights, NT, preferred_element_type=F32)
    rows, count = heads_ref.shape[0], res_ref.shape[0]
    at_row = lax.broadcasted_iota(jnp.int32, (rows, count), 0)
    at_res = lax.broadcasted_iota(jnp.int32, (rows, count), 1)
    here = jnp.where(at_row == at_res + first_ref[0], 1.0, 0.0).astype(BF)
    terms = terms + jnp.dot(here, res_ref[...], preferred_element_type=F32)
    out_ref[...] = terms.astype(BF)


def ff_kernel(mid_ref, gain_ref, g1_ref, g2_ref, u1_ref, u2_ref, out_ref):
    wide = mid_ref[...].astype(F32)
    squares = jnp.sum(wide * wide, axis=1, keepdims=True)
    high = squares.astype(BF).astype(F32)
    gained = (wide * gain_ref[...].astype(F32)).astype(BF)
    terms = []
    for a_ref, b_ref in ((g1_ref, g2_ref), (u1_ref, u2_ref)):
        weights = jnp.concatenate([a_ref[...], b_ref[...]], axis=0)
        terms.append(jnp.dot(gained, weights, preferred_element_type=F32))
    terms = jnp.concatenate(terms, axis=1)
    parts, tiles = out_ref.shape[0], terms.shape[1] // LANES
    rows = terms.shape[0] // parts
    for q in range(parts):
        mine = slice(q * rows, (q + 1) * rows)
        pack(out_ref, q, terms[mine], high[mine], (squares - high)[mine])


def pack(out_ref, q, terms, high, low):
    rows, tiles = terms.shape[0], terms.shape[1] // LANES
    for t in range(tiles):
        tile = terms[:, t * LANES : (t + 1) * LANES]
        out_ref[q, t * rows : (t + 1) * rows, :] = tile.astype(BF)
    lane = lax.broadcasted_iota(jnp.int32, (16, LANES), 1)
    extra = jnp.zeros((16, LANES), F32)
    for g in range(rows // 16):
        mine = slice(16 * g, 16 * g + 16)
        extra = jnp.where(lane == 2 * g, high[mine], extra)
        extra = jnp.where(lane == 2 * g + 1, low[mine], extra)
    out_ref[q, tiles * rows : tiles * rows + 16, :] = extra.astype(BF)


def down_kernel(pick_ref, hidden_ref, w_ref, out_ref):
    half = out_ref.shape[0]
    whole, rows = w_ref.shape[1] // LANES, 64
    blocks = []
    for q in range(hidden_ref.shape[0]):
        tiles = [hidden_ref[q, t * rows : (t + 1) * rows, :] for t in range(whole)]
        rest = hidden_ref[q, whole * rows :, :]
        rest = jnp.concatenate([rest[:, : LANES // 2], rest[:, LANES // 2 :]], axis=0)
        blocks.append(jnp.concatenate(tiles + [rest], axis=1))
    hidden = jnp.concatenate(blocks, axis=0)
    parts = []
    for k in range(2):
        pick = pick_ref[k * half : (k + 1) * half]
        rows = jnp.dot(pick, hidden, preferred_element_type=F32).astype(BF)
        parts.append(lax.dot_general(rows, w_ref[...], NT, preferred_element_type=F32))
    out_ref[...] = jnp.concatenate(parts, axis=1).astype(BF)


def mid_kernel(got_ref, out_ref):
    total = got_ref[0].astype(F32)
    for k in range(1, got_ref.shape[0]):
        total = total + got_ref[k].astype(F32)
    total = total.astype(BF)
    for k in range(out_ref.shape[0]):
        out_ref[k] = total


def hidden_kernel(mine_ref, theirs_ref, out_ref):
    sums = mine_ref[...] + theirs_ref[...].astype(F32)
    tiles = sums.shape[0] // 64
    rows = 64
    extra = sums[tiles * rows :]
    squares = jnp.concatenate(
        [
            extra[:, 2 * g : 2 * g + 1] + extra[:, 2 * g + 1 : 2 * g + 2]
            for g in range(rows // 16)
        ],
        axis=0,
    )
    scale = lax.rsqrt(squares / D + 1e-06)
    both = jnp.concatenate([sums[t * rows : (t + 1) * rows] for t in range(tiles)], axis=1)
    ff = both.shape[1] // 2
    gate = both[:, :ff] * scale
    upper = both[:, ff:] * scale
    hidden = (gate / (1.0 + jnp.exp(-gate)) * upper).astype(BF)
    whole = ff // LANES
    rest = hidden[:, whole * LANES :]
    rest = jnp.concatenate([rest[: rows // 2], rest[rows // 2 :]], axis=1)
    for q in range(out_ref.shape[0]):
        for t in range(whole):
            tile = hidden[:, t * LANES : (t + 1) * LANES]
            out_ref[q, t * rows : (t + 1) * rows, :] = tile
        out_ref[q, whole * rows :, :] = rest


def attend_kernel(length_ref, queries_hbm, new_hbm, cache_hbm, out_ref, *scratch):
    held, queries_ref, new_ref, sems = scratch
    positions, piece = held.shape[1], 512
    first = pltpu.make_async_copy(queries_hbm, queries_ref, sems.at[0])
    second = pltpu.make_async_copy(new_hbm, new_ref, sems.at[1])
    first.start()
    second.start()
    copies = []
    for k, start in enumerate(range(0, positions, piece)):
        at = (slice(None), pl.ds(start, min(piece, positions - start)))
        copies.append(pltpu.make_async_copy(cache_hbm.at[at], held.at[at], sems.at[k + 2]))
        copies[-1].start()
    first.wait()
    second.wait()
    factor = (HD + ROPE) ** (-0.5)
    queries = queries_ref[...].T
    new = new_ref[...].astype(F32)
    own = jnp.sum(queries.astype(F32) * new, axis=1, keepdims=True) * factor
    scores, highest = [], own
    for k, start in enumerate(range(0, positions, piece)):
        size = min(piece, positions - start)
        copies[k].wait()
        part = jnp.dot(queries, held[:, start : start + size], preferred_element_type=F32)
        place = lax.broadcasted_iota(jnp.int32, (1, size), 1) + start
        part = jnp.where(place < length_ref[0], part * factor, -jnp.inf)
        scores.append(part)
        highest = jnp.maximum(highest, jnp.max(part, axis=1, keepdims=True))
    total = jnp.exp(own - highest)
    expos = [jnp.exp(part - highest) for part in scores]
    for expo in expos:
        total = total + jnp.sum(expo, axis=1, keepdims=True)
    share = 1.0 / total
    own = (jnp.exp(own - highest) * share).astype(BF).astype(F32)
    probs = jnp.concatenate([(expo * share).astype(BF) for expo in expos], axis=1)
    latent = lax.dot_general(probs, held[:LAT, :], NT, preferred_element_type=F32)
    latent = latent + own * new[:, :LAT]
    count, heads = out_ref.shape[0] // 2, out_ref.shape[1]
    latent = latent.reshape(count, heads, LAT).astype(BF)
    out_ref[:count] = latent
    out_ref[count:] = latent


def exchange(array, axis, groups):
    return lax.all_to_all(
        array, axis, split_axis=0, concat_axis=0, axis_index_groups=groups, tiled=True
    )


def sum_scatter(terms, axis, count, groups=None):
    return add_blocks(exchange(terms, axis, groups), count)


def add_blocks(got, count):
    got = got.reshape((count, got.shape[0] // count) + got.shape[1:])
    return jnp.sum(got.astype(F32), axis=0)


def gather_rows(rows, axis, count, groups=None):
    copies = jnp.broadcast_to(rows[None], (count,) + rows.shape)
    got = exchange(copies, axis, groups)
    return got.reshape((count * rows.shape[0],) + rows.shape[1:])


def local(
    queries,
    latent_cache,
    new_latent,
    lengths,
    order,
    value_up,
    out_proj,
    residual,
    norm_gain,
    gate_weight,
    up_weight,
    down_weight,
    n_dp,
    n_tp,
):
    core = lax.rem(lax.axis_index("dp"), 2)
    swap = [(i, i ^ 1) for i in range(n_dp)]
    n_x = n_dp // 4
    tp = lax.axis_index("tp")

    def at(y, x, c):
        return (y * n_x + x) * 2 + c

    xs, two = range(n_x), range(2)
    along_x = [[at(y, x, c) for x in xs] for y in two for c in two]
    same_y = [[at(y, x, c) for x in xs for c in two] for y in two]
    across_y = [(i, (i + n_dp // 2) % n_dp) for i in range(n_dp)]
    out_proj2 = lax.ppermute(out_proj, "dp", swap)
    norm_gain2 = lax.ppermute(norm_gain, "dp", swap)
    residual2 = lax.ppermute(residual, "dp", swap)
    positions = latent_cache.shape[1]
    copies = pl.pallas_call(
        attend_kernel,
        out_shape=jax.ShapeDtypeStruct((2 * n_tp, queries.shape[1] // n_tp, LAT), BF),
        in_specs=[SMEM] + [pl.BlockSpec(memory_space=pltpu.HBM)] * 3,
        out_specs=VMEM,
        scratch_shapes=[
            pltpu.VMEM((LAT + ROPE, positions), BF),
            pltpu.VMEM((LAT + ROPE, queries.shape[1]), BF),
            pltpu.VMEM((1, LAT + ROPE), BF),
            pltpu.SemaphoreType.DMA(((positions + 511) // 512 + 2,)),
        ],
        compiler_params=pltpu.CompilerParams(vmem_limit_bytes=63 * 2**20 + 15 * 2**16),
    )(lengths, queries[0].T, new_latent, latent_cache[0].T)
    both_y = [
        [at(y, x, c) * n_tp + j for y in two for j in range(n_tp)] for x in xs for c in two
    ]
    heads, _, size = value_up.shape
    copies, value_up = lax.optimization_barrier((copies, value_up))
    owned = exchange(copies, ("dp", "tp"), both_y)
    maps = value_up.transpose(1, 0, 2).reshape(LAT, heads * size)
    owned, maps = lax.optimization_barrier((owned, maps))
    copies = call(
        value_kernel,
        jax.ShapeDtypeStruct((n_x, owned.shape[0], heads * size), BF),
        [VMEM] * 2,
        2 * owned.size * heads * size,
    )(owned, maps)
    heads_set = exchange(copies, "dp", along_x).reshape(-1, heads * size)
    places = jnp.arange(n_dp // 2 * n_tp)
    set_dp = (places // n_tp % 2 * n_x + places // (2 * n_tp)) * 2
    set_rows = set_dp * n_tp + places % n_tp
    count = residual.shape[0]
    res_row = tp * count
    res_dp = lax.div(res_row, n_tp)
    res_x, res_y = lax.rem(lax.div(res_dp, 2), n_x), lax.div(res_dp, 2 * n_x)
    first = (res_x * 2 + res_y) * n_tp + lax.rem(res_row, n_tp)
    first = jnp.where(lax.rem(res_dp, 2) == core, first, -count).reshape(1)
    res_pair = jnp.concatenate([residual, residual2], axis=1)
    attn_terms = call(
        attn_kernel,
        jax.ShapeDtypeStruct((heads_set.shape[0], res_pair.shape[1]), BF),
        [SMEM] + [VMEM] * 4,
        2 * heads_set.size * res_pair.shape[1],
    )(first, heads_set, out_proj.T, out_proj2.T, res_pair)
    width = residual.shape[1]
    attn_terms, gate_weight, up_weight = lax.optimization_barrier(
        (attn_terms, gate_weight, up_weight)
    )
    got = exchange(attn_terms, "tp", None)
    gate_weight2 = lax.ppermute(gate_weight, "dp", swap)
    up_weight2 = lax.ppermute(up_weight, "dp", swap)
    got, gate_weight2, up_weight2 = lax.optimization_barrier((got, gate_weight2, up_weight2))
    got = got.reshape(n_tp, -1, got.shape[1])
    copies = call(mid_kernel, jax.ShapeDtypeStruct(got.shape, BF), [VMEM], got.size)(got)
    mid_set = exchange(copies, "tp", None).reshape(-1, got.shape[2])
    mid_here, mid_there = mid_set[:, :width], mid_set[:, width:]
    gain = jnp.concatenate([norm_gain, norm_gain2])[None, :]
    ff = gate_weight.shape[1]
    tall = mid_set.shape[0] // n_x * (2 * ff // LANES) + 16
    terms = call(
        ff_kernel,
        jax.ShapeDtypeStruct((n_x, tall, LANES), BF),
        [VMEM] * 6,
        4 * mid_set.size * ff,
    )(mid_set, gain, gate_weight, gate_weight2, up_weight, up_weight2)
    terms, mid_there = lax.optimization_barrier((terms, mid_there))
    got = exchange(terms, "dp", along_x).reshape(-1, LANES)
    mid_rest = lax.ppermute(mid_there, "dp", swap)
    got, mid_rest = lax.optimization_barrier((got, mid_rest))
    sums = add_blocks(got, n_x)
    theirs = lax.ppermute(sums.astype(BF), "dp", across_y)
    copies = call(
        hidden_kernel,
        jax.ShapeDtypeStruct((n_x * 2, 2 * n_tp * ff // LANES, LANES), BF),
        [VMEM] * 2,
        8 * sums.size,
    )(sums, theirs)
    copies, order = lax.optimization_barrier((copies, order))
    hidden = exchange(copies, "dp", same_y)
    rows = n_dp * n_tp
    spots = jnp.arange(rows)
    spot_dp = at(spots // n_tp % 2, spots // (4 * n_tp), spots // (2 * n_tp) % 2)
    spot_rows = spot_dp * n_tp + spots % n_tp
    own_count = rows // n_tp
    listed = order.reshape(n_tp, 2, own_count // 2).swapaxes(0, 1).reshape(rows)
    pick = (listed[:, None] == spot_rows[None, :]).astype(BF)
    hidden, pick = lax.optimization_barrier((hidden, pick))
    width = down_weight.shape[1]
    ffn_terms = call(
        down_kernel,
        jax.ShapeDtypeStruct((rows // 2, 2 * width), BF),
        [VMEM] * 3,
        2 * rows * ff * (rows + width),
    )(pick, hidden, down_weight.T)
    ffn_own = sum_scatter(ffn_terms, "tp", n_tp)
    ffn_own = jnp.concatenate([ffn_own[:, :width], ffn_own[:, width:]], axis=0)
    wanted = lax.dynamic_slice_in_dim(order, tp * own_count, own_count)
    pick1 = (wanted[:, None] == (set_rows + core * n_tp)[None, :]).astype(BF)
    pick2 = (wanted[:, None] == (set_rows + (1 - core) * n_tp)[None, :]).astype(BF)
    mid_rows = jnp.dot(pick1, mid_here, preferred_element_type=F32) + jnp.dot(
        pick2, mid_rest, preferred_element_type=F32
    )
    return (mid_rows + ffn_own).astype(BF)


def solution(mesh):
    n_dp, n_tp = mesh.shape["dp"], mesh.shape["tp"]

    def run(*args):
        return local(*args, n_dp=n_dp, n_tp=n_tp)

    placed = (
        P(("dp", "tp"), None, None),
        P(("dp", "tp"), None, None),
        P(("dp", "tp"), None),
        P(("dp", "tp")),
        P(),
        P("tp", None, None),
        P("tp", "dp"),
        P("tp", "dp"),
        P("dp"),
        P("dp", "tp"),
        P("dp", "tp"),
        P("tp", "dp"),
    )
    return jax.shard_map(
        run, mesh=mesh, in_specs=placed, out_specs=P("tp", "dp"), check_vma=False
    )
```

```python
import jax
import jax.numpy as jnp
from jax import lax
from jax.experimental import pallas as pl
from jax.experimental.pallas import tpu as pltpu
from jax.sharding import PartitionSpec as P

D = 7168
LANES = 128
LAT = 512
ROPE = 64
HD = 128
BF = jnp.bfloat16
F32 = jnp.float32


NT = (((1,), (1,)), ((), ()))
VMEM = pl.BlockSpec(memory_space=pltpu.VMEM)
SMEM = pl.BlockSpec(memory_space=pltpu.SMEM)


def call(kernel, out, specs, flops):
    return pl.pallas_call(
        kernel,
        out_shape=out,
        in_specs=specs,
        out_specs=VMEM,
        compiler_params=pltpu.CompilerParams(vmem_limit_bytes=24 * 2**20),
        cost_estimate=pl.CostEstimate(flops=flops, bytes_accessed=2**21, transcendentals=0),
    )


def value_kernel(owned_ref, w_ref, out_ref):
    rows, heads, lat = owned_ref.shape
    size = w_ref.shape[1] // heads
    owned = owned_ref[...].reshape(rows * heads, lat)
    full = jnp.dot(owned, w_ref[...], preferred_element_type=F32)
    shape = (rows * heads, heads * size)
    head = lax.rem(lax.broadcasted_iota(jnp.int32, shape, 0), heads)
    block = lax.div(lax.broadcasted_iota(jnp.int32, shape, 1), size)
    full = jnp.where(head == block, full, 0.0).astype(BF)
    at_row = lax.broadcasted_iota(jnp.int32, (rows, rows * heads), 0)
    source = lax.div(lax.broadcasted_iota(jnp.int32, (rows, rows * heads), 1), heads)
    join = jnp.where(at_row == source, 1.0, 0.0).astype(BF)
    values = jnp.dot(join, full, preferred_element_type=F32).astype(BF)
    for q in range(out_ref.shape[0]):
        out_ref[q] = values


def attn_kernel(first_ref, heads_ref, w1_ref, w2_ref, res_ref, out_ref):
    weights = jnp.concatenate([w1_ref[...], w2_ref[...]], axis=0)
    terms = lax.dot_general(heads_ref[...], weights, NT, preferred_element_type=F32)
    rows, count = heads_ref.shape[0], res_ref.shape[0]
    at_row = lax.broadcasted_iota(jnp.int32, (rows, count), 0)
    at_res = lax.broadcasted_iota(jnp.int32, (rows, count), 1)
    here = jnp.where(at_row == at_res + first_ref[0], 1.0, 0.0).astype(BF)
    terms = terms + jnp.dot(here, res_ref[...], preferred_element_type=F32)
    out_ref[...] = terms.astype(BF)


def ff_kernel(mid_ref, gain_ref, g1_ref, g2_ref, u1_ref, u2_ref, out_ref):
    wide = mid_ref[...].astype(F32)
    squares = jnp.sum(wide * wide, axis=1, keepdims=True)
    high = squares.astype(BF).astype(F32)
    gained = (wide * gain_ref[...].astype(F32)).astype(BF)
    terms = []
    for a_ref, b_ref in ((g1_ref, g2_ref), (u1_ref, u2_ref)):
        weights = jnp.concatenate([a_ref[...], b_ref[...]], axis=0)
        terms.append(jnp.dot(gained, weights, preferred_element_type=F32))
    terms = jnp.concatenate(terms, axis=1)
    parts, tiles = out_ref.shape[0], terms.shape[1] // LANES
    rows = terms.shape[0] // parts
    for q in range(parts):
        mine = slice(q * rows, (q + 1) * rows)
        pack(out_ref, q, terms[mine], high[mine], (squares - high)[mine])


def pack(out_ref, q, terms, high, low):
    rows, tiles = terms.shape[0], terms.shape[1] // LANES
    for t in range(tiles):
        tile = terms[:, t * LANES : (t + 1) * LANES]
        out_ref[q, t * rows : (t + 1) * rows, :] = tile.astype(BF)
    lane = lax.broadcasted_iota(jnp.int32, (16, LANES), 1)
    extra = jnp.zeros((16, LANES), F32)
    for g in range(rows // 16):
        mine = slice(16 * g, 16 * g + 16)
        extra = jnp.where(lane == 2 * g, high[mine], extra)
        extra = jnp.where(lane == 2 * g + 1, low[mine], extra)
    out_ref[q, tiles * rows : tiles * rows + 16, :] = extra.astype(BF)


def down_kernel(pick_ref, hidden_ref, w_ref, out_ref):
    half = out_ref.shape[0]
    whole, rows = w_ref.shape[1] // LANES, 64
    blocks = []
    for q in range(hidden_ref.shape[0]):
        tiles = [hidden_ref[q, t * rows : (t + 1) * rows, :] for t in range(whole)]
        rest = hidden_ref[q, whole * rows :, :]
        rest = jnp.concatenate([rest[:, : LANES // 2], rest[:, LANES // 2 :]], axis=0)
        blocks.append(jnp.concatenate(tiles + [rest], axis=1))
    hidden = jnp.concatenate(blocks, axis=0)
    terms = lax.dot_general(hidden, w_ref[...], NT, preferred_element_type=F32).astype(BF)
    parts = [
        jnp.dot(pick_ref[k * half : (k + 1) * half], terms, preferred_element_type=F32)
        for k in range(2)
    ]
    out_ref[...] = jnp.concatenate(parts, axis=1).astype(BF)


def mid_kernel(got_ref, out_ref):
    total = got_ref[0].astype(F32)
    for k in range(1, got_ref.shape[0]):
        total = total + got_ref[k].astype(F32)
    total = total.astype(BF)
    for k in range(out_ref.shape[0]):
        out_ref[k] = total


def hidden_kernel(mine_ref, theirs_ref, out_ref):
    sums = mine_ref[...] + theirs_ref[...].astype(F32)
    tiles = sums.shape[0] // 64
    rows = 64
    extra = sums[tiles * rows :]
    squares = jnp.concatenate(
        [
            extra[:, 2 * g : 2 * g + 1] + extra[:, 2 * g + 1 : 2 * g + 2]
            for g in range(rows // 16)
        ],
        axis=0,
    )
    scale = lax.rsqrt(squares / D + 1e-06)
    both = jnp.concatenate([sums[t * rows : (t + 1) * rows] for t in range(tiles)], axis=1)
    ff = both.shape[1] // 2
    gate = both[:, :ff] * scale
    upper = both[:, ff:] * scale
    hidden = (gate / (1.0 + jnp.exp(-gate)) * upper).astype(BF)
    whole = ff // LANES
    rest = hidden[:, whole * LANES :]
    rest = jnp.concatenate([rest[: rows // 2], rest[rows // 2 :]], axis=1)
    for q in range(out_ref.shape[0]):
        for t in range(whole):
            tile = hidden[:, t * LANES : (t + 1) * LANES]
            out_ref[q, t * rows : (t + 1) * rows, :] = tile
        out_ref[q, whole * rows :, :] = rest


def attend_kernel(length_ref, queries_hbm, new_hbm, cache_hbm, out_ref, *scratch):
    held, queries_ref, new_ref, sems = scratch
    positions, piece = held.shape[1], 512
    first = pltpu.make_async_copy(queries_hbm, queries_ref, sems.at[0])
    second = pltpu.make_async_copy(new_hbm, new_ref, sems.at[1])
    first.start()
    second.start()
    copies = []
    for k, start in enumerate(range(0, positions, piece)):
        at = (slice(None), pl.ds(start, min(piece, positions - start)))
        copies.append(pltpu.make_async_copy(cache_hbm.at[at], held.at[at], sems.at[k + 2]))
        copies[-1].start()
    first.wait()
    second.wait()
    factor = (HD + ROPE) ** (-0.5)
    queries = queries_ref[...].T
    new = new_ref[...].astype(F32)
    own = jnp.sum(queries.astype(F32) * new, axis=1, keepdims=True) * factor
    scores, highest = [], own
    for k, start in enumerate(range(0, positions, piece)):
        size = min(piece, positions - start)
        copies[k].wait()
        part = jnp.dot(queries, held[:, start : start + size], preferred_element_type=F32)
        place = lax.broadcasted_iota(jnp.int32, (1, size), 1) + start
        part = jnp.where(place < length_ref[0], part * factor, -jnp.inf)
        scores.append(part)
        highest = jnp.maximum(highest, jnp.max(part, axis=1, keepdims=True))
    total = jnp.exp(own - highest)
    expos = [jnp.exp(part - highest) for part in scores]
    for expo in expos:
        total = total + jnp.sum(expo, axis=1, keepdims=True)
    share = 1.0 / total
    own = (jnp.exp(own - highest) * share).astype(BF).astype(F32)
    probs = jnp.concatenate([(expo * share).astype(BF) for expo in expos], axis=1)
    latent = lax.dot_general(held[:LAT, :], probs, NT, preferred_element_type=F32)
    latent = latent.T + own * new[:, :LAT]
    count, heads = out_ref.shape[0] // 2, out_ref.shape[1]
    latent = latent.reshape(count, heads, LAT).astype(BF)
    out_ref[:count] = latent
    out_ref[count:] = latent


def exchange(array, axis, groups):
    return lax.all_to_all(
        array, axis, split_axis=0, concat_axis=0, axis_index_groups=groups, tiled=True
    )


def sum_scatter(terms, axis, count, groups=None):
    return add_blocks(exchange(terms, axis, groups), count)


def add_blocks(got, count):
    got = got.reshape((count, got.shape[0] // count) + got.shape[1:])
    return jnp.sum(got.astype(F32), axis=0)


def gather_rows(rows, axis, count, groups=None):
    copies = jnp.broadcast_to(rows[None], (count,) + rows.shape)
    got = exchange(copies, axis, groups)
    return got.reshape((count * rows.shape[0],) + rows.shape[1:])


def local(
    queries,
    latent_cache,
    new_latent,
    lengths,
    order,
    value_up,
    out_proj,
    residual,
    norm_gain,
    gate_weight,
    up_weight,
    down_weight,
    n_dp,
    n_tp,
):
    core = lax.rem(lax.axis_index("dp"), 2)
    swap = [(i, i ^ 1) for i in range(n_dp)]
    n_x = n_dp // 4
    tp = lax.axis_index("tp")

    def at(y, x, c):
        return (y * n_x + x) * 2 + c

    xs, two = range(n_x), range(2)
    along_x = [[at(y, x, c) for x in xs] for y in two for c in two]
    same_y = [[at(y, x, c) for x in xs for c in two] for y in two]
    across_y = [(i, (i + n_dp // 2) % n_dp) for i in range(n_dp)]
    out_proj2 = lax.ppermute(out_proj, "dp", swap)
    norm_gain2 = lax.ppermute(norm_gain, "dp", swap)
    residual2 = lax.ppermute(residual, "dp", swap)
    positions = latent_cache.shape[1]
    copies = pl.pallas_call(
        attend_kernel,
        out_shape=jax.ShapeDtypeStruct((2 * n_tp, queries.shape[1] // n_tp, LAT), BF),
        in_specs=[SMEM] + [pl.BlockSpec(memory_space=pltpu.HBM)] * 3,
        out_specs=VMEM,
        scratch_shapes=[
            pltpu.VMEM((LAT + ROPE, positions), BF),
            pltpu.VMEM((LAT + ROPE, queries.shape[1]), BF),
            pltpu.VMEM((1, LAT + ROPE), BF),
            pltpu.SemaphoreType.DMA(((positions + 511) // 512 + 2,)),
        ],
        compiler_params=pltpu.CompilerParams(vmem_limit_bytes=63 * 2**20 + 15 * 2**16),
    )(lengths, queries[0].T, new_latent, latent_cache[0].T)
    both_y = [
        [at(y, x, c) * n_tp + j for y in two for j in range(n_tp)] for x in xs for c in two
    ]
    heads, _, size = value_up.shape
    copies, value_up = lax.optimization_barrier((copies, value_up))
    owned = exchange(copies, ("dp", "tp"), both_y)
    maps = value_up.transpose(1, 0, 2).reshape(LAT, heads * size)
    owned, maps = lax.optimization_barrier((owned, maps))
    copies = call(
        value_kernel,
        jax.ShapeDtypeStruct((n_x, owned.shape[0], heads * size), BF),
        [VMEM] * 2,
        2 * owned.size * heads * size,
    )(owned, maps)
    heads_set = exchange(copies, "dp", along_x).reshape(-1, heads * size)
    places = jnp.arange(n_dp // 2 * n_tp)
    set_dp = (places // n_tp % 2 * n_x + places // (2 * n_tp)) * 2
    set_rows = set_dp * n_tp + places % n_tp
    count = residual.shape[0]
    res_row = tp * count
    res_dp = lax.div(res_row, n_tp)
    res_x, res_y = lax.rem(lax.div(res_dp, 2), n_x), lax.div(res_dp, 2 * n_x)
    first = (res_x * 2 + res_y) * n_tp + lax.rem(res_row, n_tp)
    first = jnp.where(lax.rem(res_dp, 2) == core, first, -count).reshape(1)
    res_pair = jnp.concatenate([residual, residual2], axis=1)
    attn_terms = call(
        attn_kernel,
        jax.ShapeDtypeStruct((heads_set.shape[0], res_pair.shape[1]), BF),
        [SMEM] + [VMEM] * 4,
        2 * heads_set.size * res_pair.shape[1],
    )(first, heads_set, out_proj.T, out_proj2.T, res_pair)
    width = residual.shape[1]
    attn_terms, gate_weight, up_weight = lax.optimization_barrier(
        (attn_terms, gate_weight, up_weight)
    )
    got = exchange(attn_terms, "tp", None)
    gate_weight2 = lax.ppermute(gate_weight, "dp", swap)
    up_weight2 = lax.ppermute(up_weight, "dp", swap)
    got, gate_weight2, up_weight2 = lax.optimization_barrier((got, gate_weight2, up_weight2))
    got = got.reshape(n_tp, -1, got.shape[1])
    copies = call(mid_kernel, jax.ShapeDtypeStruct(got.shape, BF), [VMEM], got.size)(got)
    mid_set = exchange(copies, "tp", None).reshape(-1, got.shape[2])
    mid_here, mid_there = mid_set[:, :width], mid_set[:, width:]
    gain = jnp.concatenate([norm_gain, norm_gain2])[None, :]
    ff = gate_weight.shape[1]
    tall = mid_set.shape[0] // n_x * (2 * ff // LANES) + 16
    terms = call(
        ff_kernel,
        jax.ShapeDtypeStruct((n_x, tall, LANES), BF),
        [VMEM] * 6,
        4 * mid_set.size * ff,
    )(mid_set, gain, gate_weight, gate_weight2, up_weight, up_weight2)
    terms, mid_there = lax.optimization_barrier((terms, mid_there))
    got = exchange(terms, "dp", along_x).reshape(-1, LANES)
    mid_rest = lax.ppermute(mid_there, "dp", swap)
    got, mid_rest = lax.optimization_barrier((got, mid_rest))
    sums = add_blocks(got, n_x)
    theirs = lax.ppermute(sums.astype(BF), "dp", across_y)
    copies = call(
        hidden_kernel,
        jax.ShapeDtypeStruct((n_x * 2, 2 * n_tp * ff // LANES, LANES), BF),
        [VMEM] * 2,
        8 * sums.size,
    )(sums, theirs)
    copies, order = lax.optimization_barrier((copies, order))
    hidden = exchange(copies, "dp", same_y)
    rows = n_dp * n_tp
    spots = jnp.arange(rows)
    spot_dp = at(spots // n_tp % 2, spots // (4 * n_tp), spots // (2 * n_tp) % 2)
    spot_rows = spot_dp * n_tp + spots % n_tp
    own_count = rows // n_tp
    listed = order.reshape(n_tp, 2, own_count // 2).swapaxes(0, 1).reshape(rows)
    pick = (listed[:, None] == spot_rows[None, :]).astype(BF)
    hidden, pick = lax.optimization_barrier((hidden, pick))
    width = down_weight.shape[1]
    ffn_terms = call(
        down_kernel,
        jax.ShapeDtypeStruct((rows // 2, 2 * width), BF),
        [VMEM] * 3,
        2 * rows * ff * (rows + width),
    )(pick, hidden, down_weight.T)
    wanted = lax.dynamic_slice_in_dim(order, tp * own_count, own_count)
    pick1 = (wanted[:, None] == (set_rows + core * n_tp)[None, :]).astype(BF)
    pick2 = (wanted[:, None] == (set_rows + (1 - core) * n_tp)[None, :]).astype(BF)
    mid_rows = jnp.dot(pick1, mid_here, preferred_element_type=F32) + jnp.dot(
        pick2, mid_rest, preferred_element_type=F32
    )
    got = exchange(ffn_terms, "tp", None)
    got, mid_rows = lax.optimization_barrier((got, mid_rows))
    ffn_own = add_blocks(got, n_tp)
    ffn_own = jnp.concatenate([ffn_own[:, :width], ffn_own[:, width:]], axis=0)
    return (mid_rows + ffn_own).astype(BF)


def solution(mesh):
    n_dp, n_tp = mesh.shape["dp"], mesh.shape["tp"]

    def run(*args):
        return local(*args, n_dp=n_dp, n_tp=n_tp)

    placed = (
        P(("dp", "tp"), None, None),
        P(("dp", "tp"), None, None),
        P(("dp", "tp"), None),
        P(("dp", "tp")),
        P(),
        P("tp", None, None),
        P("tp", "dp"),
        P("tp", "dp"),
        P("dp"),
        P("dp", "tp"),
        P("dp", "tp"),
        P("tp", "dp"),
    )
    return jax.shard_map(
        run, mesh=mesh, in_specs=placed, out_specs=P("tp", "dp"), check_vma=False
    )
```

```python
import jax
import jax.numpy as jnp
from jax import lax
from jax.experimental import pallas as pl
from jax.experimental.pallas import tpu as pltpu
from jax.sharding import PartitionSpec as P

D = 7168
LANES = 128
LAT = 512
ROPE = 64
HD = 128
BF = jnp.bfloat16
F32 = jnp.float32


NT = (((1,), (1,)), ((), ()))
VMEM = pl.BlockSpec(memory_space=pltpu.VMEM)
SMEM = pl.BlockSpec(memory_space=pltpu.SMEM)


def call(kernel, out, specs, flops):
    return pl.pallas_call(
        kernel,
        out_shape=out,
        in_specs=specs,
        out_specs=VMEM,
        compiler_params=pltpu.CompilerParams(vmem_limit_bytes=24 * 2**20),
        cost_estimate=pl.CostEstimate(flops=flops, bytes_accessed=2**21, transcendentals=0),
    )


def value_kernel(owned_ref, w_ref, out_ref):
    rows, heads, lat = owned_ref.shape
    size = w_ref.shape[1] // heads
    owned = owned_ref[...].reshape(rows * heads, lat)
    full = jnp.dot(owned, w_ref[...], preferred_element_type=F32)
    shape = (rows * heads, heads * size)
    head = lax.rem(lax.broadcasted_iota(jnp.int32, shape, 0), heads)
    block = lax.div(lax.broadcasted_iota(jnp.int32, shape, 1), size)
    full = jnp.where(head == block, full, 0.0).astype(BF)
    at_row = lax.broadcasted_iota(jnp.int32, (rows, rows * heads), 0)
    source = lax.div(lax.broadcasted_iota(jnp.int32, (rows, rows * heads), 1), heads)
    join = jnp.where(at_row == source, 1.0, 0.0).astype(BF)
    values = jnp.dot(join, full, preferred_element_type=F32).astype(BF)
    for q in range(out_ref.shape[0]):
        out_ref[q] = values


def attn_kernel(first_ref, heads_ref, w1_ref, w2_ref, res_ref, out_ref):
    weights = jnp.concatenate([w1_ref[...], w2_ref[...]], axis=0)
    terms = lax.dot_general(heads_ref[...], weights, NT, preferred_element_type=F32)
    rows, count = heads_ref.shape[0], res_ref.shape[0]
    at_row = lax.broadcasted_iota(jnp.int32, (rows, count), 0)
    at_res = lax.broadcasted_iota(jnp.int32, (rows, count), 1)
    here = jnp.where(at_row == at_res + first_ref[0], 1.0, 0.0).astype(BF)
    terms = terms + jnp.dot(here, res_ref[...], preferred_element_type=F32)
    out_ref[...] = terms.astype(BF)


def ff_kernel(mid_ref, gain_ref, g1_ref, g2_ref, u1_ref, u2_ref, out_ref):
    wide = mid_ref[...].astype(F32)
    squares = jnp.sum(wide * wide, axis=1, keepdims=True)
    high = squares.astype(BF).astype(F32)
    gained = (wide * gain_ref[...].astype(F32)).astype(BF)
    terms = []
    for a_ref, b_ref in ((g1_ref, g2_ref), (u1_ref, u2_ref)):
        weights = jnp.concatenate([a_ref[...], b_ref[...]], axis=0)
        terms.append(jnp.dot(gained, weights, preferred_element_type=F32))
    terms = jnp.concatenate(terms, axis=1)
    parts, tiles = out_ref.shape[0], terms.shape[1] // LANES
    rows = terms.shape[0] // parts
    for q in range(parts):
        mine = slice(q * rows, (q + 1) * rows)
        pack(out_ref, q, terms[mine], high[mine], (squares - high)[mine])


def pack(out_ref, q, terms, high, low):
    rows, tiles = terms.shape[0], terms.shape[1] // LANES
    for t in range(tiles):
        tile = terms[:, t * LANES : (t + 1) * LANES]
        out_ref[q, t * rows : (t + 1) * rows, :] = tile.astype(BF)
    lane = lax.broadcasted_iota(jnp.int32, (16, LANES), 1)
    extra = jnp.zeros((16, LANES), F32)
    for g in range(rows // 16):
        mine = slice(16 * g, 16 * g + 16)
        extra = jnp.where(lane == 2 * g, high[mine], extra)
        extra = jnp.where(lane == 2 * g + 1, low[mine], extra)
    out_ref[q, tiles * rows : tiles * rows + 16, :] = extra.astype(BF)


def down_kernel(pick_ref, hidden_ref, w_ref, out_ref):
    half = out_ref.shape[0]
    whole, rows = w_ref.shape[1] // LANES, 64
    blocks = []
    for q in range(hidden_ref.shape[0]):
        tiles = [hidden_ref[q, t * rows : (t + 1) * rows, :] for t in range(whole)]
        rest = hidden_ref[q, whole * rows :, :]
        rest = jnp.concatenate([rest[:, : LANES // 2], rest[:, LANES // 2 :]], axis=0)
        blocks.append(jnp.concatenate(tiles + [rest], axis=1))
    hidden = jnp.concatenate(blocks, axis=0)
    terms = lax.dot_general(hidden, w_ref[...], NT, preferred_element_type=F32).astype(BF)
    parts = [
        jnp.dot(pick_ref[k * half : (k + 1) * half], terms, preferred_element_type=F32)
        for k in range(2)
    ]
    out_ref[...] = jnp.concatenate(parts, axis=1).astype(BF)


def mid_kernel(got_ref, out_ref):
    total = got_ref[0].astype(F32)
    for k in range(1, got_ref.shape[0]):
        total = total + got_ref[k].astype(F32)
    total = total.astype(BF)
    for k in range(out_ref.shape[0]):
        out_ref[k] = total


def hidden_kernel(sums_ref, out_ref):
    sums = sums_ref[0].astype(F32) + sums_ref[1].astype(F32)
    tiles = sums.shape[0] // 64
    rows = 64
    extra = sums[tiles * rows :]
    squares = jnp.concatenate(
        [
            extra[:, 2 * g : 2 * g + 1] + extra[:, 2 * g + 1 : 2 * g + 2]
            for g in range(rows // 16)
        ],
        axis=0,
    )
    scale = lax.rsqrt(squares / D + 1e-06)
    both = jnp.concatenate([sums[t * rows : (t + 1) * rows] for t in range(tiles)], axis=1)
    ff = both.shape[1] // 2
    gate = both[:, :ff] * scale
    upper = both[:, ff:] * scale
    hidden = (gate / (1.0 + jnp.exp(-gate)) * upper).astype(BF)
    whole = ff // LANES
    rest = hidden[:, whole * LANES :]
    rest = jnp.concatenate([rest[: rows // 2], rest[rows // 2 :]], axis=1)
    for q in range(out_ref.shape[0]):
        for t in range(whole):
            tile = hidden[:, t * LANES : (t + 1) * LANES]
            out_ref[q, t * rows : (t + 1) * rows, :] = tile
        out_ref[q, whole * rows :, :] = rest


def attend_kernel(length_ref, queries_hbm, new_hbm, cache_hbm, out_ref, *scratch):
    held, queries_ref, new_ref, sems = scratch
    positions, piece = held.shape[1], 512
    first = pltpu.make_async_copy(queries_hbm, queries_ref, sems.at[0])
    second = pltpu.make_async_copy(new_hbm, new_ref, sems.at[1])
    first.start()
    second.start()
    copies = []
    for k, start in enumerate(range(0, positions, piece)):
        at = (slice(None), pl.ds(start, min(piece, positions - start)))
        copies.append(pltpu.make_async_copy(cache_hbm.at[at], held.at[at], sems.at[k + 2]))
        copies[-1].start()
    first.wait()
    second.wait()
    factor = (HD + ROPE) ** (-0.5)
    queries = queries_ref[...].T
    new = new_ref[...].astype(F32)
    own = jnp.sum(queries.astype(F32) * new, axis=1, keepdims=True) * factor
    scores, highest = [], own
    for k, start in enumerate(range(0, positions, piece)):
        size = min(piece, positions - start)
        copies[k].wait()
        part = jnp.dot(queries, held[:, start : start + size], preferred_element_type=F32)
        place = lax.broadcasted_iota(jnp.int32, (1, size), 1) + start
        part = jnp.where(place < length_ref[0], part * factor, -jnp.inf)
        scores.append(part)
        highest = jnp.maximum(highest, jnp.max(part, axis=1, keepdims=True))
    total = jnp.exp(own - highest)
    expos = [jnp.exp(part - highest) for part in scores]
    for expo in expos:
        total = total + jnp.sum(expo, axis=1, keepdims=True)
    share = 1.0 / total
    own = (jnp.exp(own - highest) * share).astype(BF).astype(F32)
    probs = jnp.concatenate([(expo * share).astype(BF) for expo in expos], axis=1)
    latent = lax.dot_general(held[:LAT, :], probs, NT, preferred_element_type=F32)
    latent = latent.T + own * new[:, :LAT]
    count, heads = out_ref.shape[0] // 2, out_ref.shape[1]
    latent = latent.reshape(count, heads, LAT).astype(BF)
    out_ref[:count] = latent
    out_ref[count:] = latent


def exchange(array, axis, groups):
    return lax.all_to_all(
        array, axis, split_axis=0, concat_axis=0, axis_index_groups=groups, tiled=True
    )


def sum_scatter(terms, axis, count, groups=None):
    return add_blocks(exchange(terms, axis, groups), count)


def add_blocks(got, count):
    got = got.reshape((count, got.shape[0] // count) + got.shape[1:])
    return jnp.sum(got.astype(F32), axis=0)


def gather_rows(rows, axis, count, groups=None):
    copies = jnp.broadcast_to(rows[None], (count,) + rows.shape)
    got = exchange(copies, axis, groups)
    return got.reshape((count * rows.shape[0],) + rows.shape[1:])


def local(
    queries,
    latent_cache,
    new_latent,
    lengths,
    order,
    value_up,
    out_proj,
    residual,
    norm_gain,
    gate_weight,
    up_weight,
    down_weight,
    n_dp,
    n_tp,
):
    core = lax.rem(lax.axis_index("dp"), 2)
    swap = [(i, i ^ 1) for i in range(n_dp)]
    n_x = n_dp // 4
    tp = lax.axis_index("tp")

    def at(y, x, c):
        return (y * n_x + x) * 2 + c

    xs, two = range(n_x), range(2)
    along_x = [[at(y, x, c) for x in xs] for y in two for c in two]
    same_y = [[at(y, x, c) for x in xs for c in two] for y in two]
    along_y = [[at(y, x, c) for y in two] for x in xs for c in two]
    out_proj2 = lax.ppermute(out_proj, "dp", swap)
    norm_gain2 = lax.ppermute(norm_gain, "dp", swap)
    residual2 = lax.ppermute(residual, "dp", swap)
    positions = latent_cache.shape[1]
    copies = pl.pallas_call(
        attend_kernel,
        out_shape=jax.ShapeDtypeStruct((2 * n_tp, queries.shape[1] // n_tp, LAT), BF),
        in_specs=[SMEM] + [pl.BlockSpec(memory_space=pltpu.HBM)] * 3,
        out_specs=VMEM,
        scratch_shapes=[
            pltpu.VMEM((LAT + ROPE, positions), BF),
            pltpu.VMEM((LAT + ROPE, queries.shape[1]), BF),
            pltpu.VMEM((1, LAT + ROPE), BF),
            pltpu.SemaphoreType.DMA(((positions + 511) // 512 + 2,)),
        ],
        compiler_params=pltpu.CompilerParams(vmem_limit_bytes=63 * 2**20 + 15 * 2**16),
    )(lengths, queries[0].T, new_latent, latent_cache[0].T)
    both_y = [
        [at(y, x, c) * n_tp + j for y in two for j in range(n_tp)] for x in xs for c in two
    ]
    heads, _, size = value_up.shape
    copies, value_up = lax.optimization_barrier((copies, value_up))
    owned = exchange(copies, ("dp", "tp"), both_y)
    maps = value_up.transpose(1, 0, 2).reshape(LAT, heads * size)
    owned, maps = lax.optimization_barrier((owned, maps))
    copies = call(
        value_kernel,
        jax.ShapeDtypeStruct((n_x, owned.shape[0], heads * size), BF),
        [VMEM] * 2,
        2 * owned.size * heads * size,
    )(owned, maps)
    heads_set = exchange(copies, "dp", along_x).reshape(-1, heads * size)
    places = jnp.arange(n_dp // 2 * n_tp)
    set_dp = (places // n_tp % 2 * n_x + places // (2 * n_tp)) * 2
    set_rows = set_dp * n_tp + places % n_tp
    count = residual.shape[0]
    res_row = tp * count
    res_dp = lax.div(res_row, n_tp)
    res_x, res_y = lax.rem(lax.div(res_dp, 2), n_x), lax.div(res_dp, 2 * n_x)
    first = (res_x * 2 + res_y) * n_tp + lax.rem(res_row, n_tp)
    first = jnp.where(lax.rem(res_dp, 2) == core, first, -count).reshape(1)
    res_pair = jnp.concatenate([residual, residual2], axis=1)
    attn_terms = call(
        attn_kernel,
        jax.ShapeDtypeStruct((heads_set.shape[0], res_pair.shape[1]), BF),
        [SMEM] + [VMEM] * 4,
        2 * heads_set.size * res_pair.shape[1],
    )(first, heads_set, out_proj.T, out_proj2.T, res_pair)
    width = residual.shape[1]
    attn_terms, gate_weight, up_weight = lax.optimization_barrier(
        (attn_terms, gate_weight, up_weight)
    )
    got = exchange(attn_terms, "tp", None)
    gate_weight2 = lax.ppermute(gate_weight, "dp", swap)
    up_weight2 = lax.ppermute(up_weight, "dp", swap)
    got, gate_weight2, up_weight2 = lax.optimization_barrier((got, gate_weight2, up_weight2))
    got = got.reshape(n_tp, -1, got.shape[1])
    copies = call(mid_kernel, jax.ShapeDtypeStruct(got.shape, BF), [VMEM], got.size)(got)
    mid_set = exchange(copies, "tp", None).reshape(-1, got.shape[2])
    mid_here, mid_there = mid_set[:, :width], mid_set[:, width:]
    gain = jnp.concatenate([norm_gain, norm_gain2])[None, :]
    ff = gate_weight.shape[1]
    tall = mid_set.shape[0] // n_x * (2 * ff // LANES) + 16
    terms = call(
        ff_kernel,
        jax.ShapeDtypeStruct((n_x, tall, LANES), BF),
        [VMEM] * 6,
        4 * mid_set.size * ff,
    )(mid_set, gain, gate_weight, gate_weight2, up_weight, up_weight2)
    terms, mid_there = lax.optimization_barrier((terms, mid_there))
    got = exchange(terms, "dp", along_x).reshape(-1, LANES)
    mid_rest = lax.ppermute(mid_there, "dp", swap)
    got, mid_rest = lax.optimization_barrier((got, mid_rest))
    sums = add_blocks(got, n_x).astype(BF)
    sums = jnp.broadcast_to(sums, (2,) + sums.shape)
    sums, order = lax.optimization_barrier((sums, order))
    sums = exchange(sums, "dp", along_y)
    rows = n_dp * n_tp
    own_count = rows // n_tp
    spots = jnp.arange(rows)
    spot_dp = at(spots // n_tp % 2, spots // (4 * n_tp), spots // (2 * n_tp) % 2)
    spot_rows = spot_dp * n_tp + spots % n_tp
    listed = order.reshape(n_tp, 2, own_count // 2).swapaxes(0, 1).reshape(rows)
    pick = (listed[:, None] == spot_rows[None, :]).astype(BF)
    sums, pick = lax.optimization_barrier((sums, pick))
    copies = call(
        hidden_kernel,
        jax.ShapeDtypeStruct((n_x * 2, 2 * n_tp * ff // LANES, LANES), BF),
        [VMEM],
        8 * sums.size,
    )(sums)
    wanted = lax.dynamic_slice_in_dim(order, tp * own_count, own_count)
    pick1 = (wanted[:, None] == (set_rows + core * n_tp)[None, :]).astype(BF)
    pick2 = (wanted[:, None] == (set_rows + (1 - core) * n_tp)[None, :]).astype(BF)
    copies, mid_here = lax.optimization_barrier((copies, mid_here))
    hidden = exchange(copies, "dp", same_y)
    mid_rows = jnp.dot(pick1, mid_here, preferred_element_type=F32)
    hidden, mid_rows = lax.optimization_barrier((hidden, mid_rows))
    width = down_weight.shape[1]
    ffn_terms = call(
        down_kernel,
        jax.ShapeDtypeStruct((rows // 2, 2 * width), BF),
        [VMEM] * 3,
        2 * rows * ff * (rows + width),
    )(pick, hidden, down_weight.T)
    ffn_terms, mid_rest = lax.optimization_barrier((ffn_terms, mid_rest))
    mid_rows = mid_rows + jnp.dot(pick2, mid_rest, preferred_element_type=F32)
    got = exchange(ffn_terms, "tp", None)
    got, mid_rows = lax.optimization_barrier((got, mid_rows))
    ffn_own = add_blocks(got, n_tp)
    ffn_own = jnp.concatenate([ffn_own[:, :width], ffn_own[:, width:]], axis=0)
    return (mid_rows + ffn_own).astype(BF)


def solution(mesh):
    n_dp, n_tp = mesh.shape["dp"], mesh.shape["tp"]

    def run(*args):
        return local(*args, n_dp=n_dp, n_tp=n_tp)

    placed = (
        P(("dp", "tp"), None, None),
        P(("dp", "tp"), None, None),
        P(("dp", "tp"), None),
        P(("dp", "tp")),
        P(),
        P("tp", None, None),
        P("tp", "dp"),
        P("tp", "dp"),
        P("dp"),
        P("dp", "tp"),
        P("dp", "tp"),
        P("tp", "dp"),
    )
    return jax.shard_map(
        run, mesh=mesh, in_specs=placed, out_specs=P("tp", "dp"), check_vma=False
    )
```

```python
import jax
import jax.numpy as jnp
from jax import lax
from jax.experimental import pallas as pl
from jax.experimental.pallas import tpu as pltpu
from jax.sharding import PartitionSpec as P

D = 7168
LANES = 128
LAT = 512
ROPE = 64
HD = 128
BF = jnp.bfloat16
F32 = jnp.float32


NT = (((1,), (1,)), ((), ()))
VMEM = pl.BlockSpec(memory_space=pltpu.VMEM)
SMEM = pl.BlockSpec(memory_space=pltpu.SMEM)


def call(kernel, out, specs, flops):
    return pl.pallas_call(
        kernel,
        out_shape=out,
        in_specs=specs,
        out_specs=VMEM,
        compiler_params=pltpu.CompilerParams(vmem_limit_bytes=24 * 2**20),
        cost_estimate=pl.CostEstimate(flops=flops, bytes_accessed=2**21, transcendentals=0),
    )


def value_kernel(owned_ref, w_ref, out_ref):
    rows, heads, lat = owned_ref.shape
    size = w_ref.shape[1] // heads
    owned = owned_ref[...].reshape(rows * heads, lat)
    full = jnp.dot(owned, w_ref[...], preferred_element_type=F32)
    shape = (rows * heads, heads * size)
    head = lax.rem(lax.broadcasted_iota(jnp.int32, shape, 0), heads)
    block = lax.div(lax.broadcasted_iota(jnp.int32, shape, 1), size)
    full = jnp.where(head == block, full, 0.0).astype(BF)
    at_row = lax.broadcasted_iota(jnp.int32, (rows, rows * heads), 0)
    source = lax.div(lax.broadcasted_iota(jnp.int32, (rows, rows * heads), 1), heads)
    join = jnp.where(at_row == source, 1.0, 0.0).astype(BF)
    values = jnp.dot(join, full, preferred_element_type=F32).astype(BF)
    for q in range(out_ref.shape[0]):
        out_ref[q] = values


def attn_kernel(first_ref, heads_ref, w1_ref, w2_ref, res_ref, out_ref):
    weights = jnp.concatenate([w1_ref[...], w2_ref[...]], axis=0)
    terms = lax.dot_general(heads_ref[...], weights, NT, preferred_element_type=F32)
    rows, count = heads_ref.shape[0], res_ref.shape[0]
    at_row = lax.broadcasted_iota(jnp.int32, (rows, count), 0)
    at_res = lax.broadcasted_iota(jnp.int32, (rows, count), 1)
    here = jnp.where(at_row == at_res + first_ref[0], 1.0, 0.0).astype(BF)
    terms = terms + jnp.dot(here, res_ref[...], preferred_element_type=F32)
    out_ref[...] = terms.astype(BF)


def ff_kernel(mid_ref, gain_ref, g1_ref, g2_ref, u1_ref, u2_ref, out_ref):
    wide = mid_ref[...].astype(F32)
    squares = jnp.sum(wide * wide, axis=1, keepdims=True)
    high = squares.astype(BF).astype(F32)
    gained = (wide * gain_ref[...].astype(F32)).astype(BF)
    terms = []
    for a_ref, b_ref in ((g1_ref, g2_ref), (u1_ref, u2_ref)):
        weights = jnp.concatenate([a_ref[...], b_ref[...]], axis=0)
        terms.append(jnp.dot(gained, weights, preferred_element_type=F32))
    terms = jnp.concatenate(terms, axis=1)
    parts, tiles = out_ref.shape[0], terms.shape[1] // LANES
    rows = terms.shape[0] // parts
    for q in range(parts):
        mine = slice(q * rows, (q + 1) * rows)
        pack(out_ref, q, terms[mine], high[mine], (squares - high)[mine])


def pack(out_ref, q, terms, high, low):
    rows, tiles = terms.shape[0], terms.shape[1] // LANES
    for t in range(tiles):
        tile = terms[:, t * LANES : (t + 1) * LANES]
        out_ref[q, t * rows : (t + 1) * rows, :] = tile.astype(BF)
    lane = lax.broadcasted_iota(jnp.int32, (16, LANES), 1)
    extra = jnp.zeros((16, LANES), F32)
    for g in range(rows // 16):
        mine = slice(16 * g, 16 * g + 16)
        extra = jnp.where(lane == 2 * g, high[mine], extra)
        extra = jnp.where(lane == 2 * g + 1, low[mine], extra)
    out_ref[q, tiles * rows : tiles * rows + 16, :] = extra.astype(BF)


def down_kernel(pick_ref, hidden_ref, w_ref, out_ref):
    half = out_ref.shape[0]
    whole, rows = w_ref.shape[1] // LANES, 64
    blocks = []
    for q in range(hidden_ref.shape[0]):
        tiles = [hidden_ref[q, t * rows : (t + 1) * rows, :] for t in range(whole)]
        rest = hidden_ref[q, whole * rows :, :]
        rest = jnp.concatenate([rest[:, : LANES // 2], rest[:, LANES // 2 :]], axis=0)
        blocks.append(jnp.concatenate(tiles + [rest], axis=1))
    hidden = jnp.concatenate(blocks, axis=0)
    terms = lax.dot_general(hidden, w_ref[...], NT, preferred_element_type=F32).astype(BF)
    parts = [
        jnp.dot(pick_ref[k * half : (k + 1) * half], terms, preferred_element_type=F32)
        for k in range(2)
    ]
    out_ref[...] = jnp.concatenate(parts, axis=1).astype(BF)


def mid_kernel(got_ref, out_ref):
    total = got_ref[0].astype(F32)
    for k in range(1, got_ref.shape[0]):
        total = total + got_ref[k].astype(F32)
    total = total.astype(BF)
    for k in range(out_ref.shape[0]):
        out_ref[k] = total


def hidden_kernel(mine_ref, theirs_ref, out_ref):
    sums = mine_ref[...] + theirs_ref[...].astype(F32)
    tiles = sums.shape[0] // 64
    rows = 64
    extra = sums[tiles * rows :]
    squares = jnp.concatenate(
        [
            extra[:, 2 * g : 2 * g + 1] + extra[:, 2 * g + 1 : 2 * g + 2]
            for g in range(rows // 16)
        ],
        axis=0,
    )
    scale = lax.rsqrt(squares / D + 1e-06)
    both = jnp.concatenate([sums[t * rows : (t + 1) * rows] for t in range(tiles)], axis=1)
    ff = both.shape[1] // 2
    gate = both[:, :ff] * scale
    upper = both[:, ff:] * scale
    hidden = (gate / (1.0 + jnp.exp(-gate)) * upper).astype(BF)
    whole = ff // LANES
    rest = hidden[:, whole * LANES :]
    rest = jnp.concatenate([rest[: rows // 2], rest[rows // 2 :]], axis=1)
    for q in range(out_ref.shape[0]):
        for t in range(whole):
            tile = hidden[:, t * LANES : (t + 1) * LANES]
            out_ref[q, t * rows : (t + 1) * rows, :] = tile
        out_ref[q, whole * rows :, :] = rest


def attend_kernel(length_ref, queries_hbm, new_hbm, cache_hbm, out_ref, *scratch):
    held, queries_ref, new_ref, sems = scratch
    positions, piece = held.shape[1], 512
    first = pltpu.make_async_copy(queries_hbm, queries_ref, sems.at[0])
    second = pltpu.make_async_copy(new_hbm, new_ref, sems.at[1])
    first.start()
    second.start()
    copies = []
    for k, start in enumerate(range(0, positions, piece)):
        at = (slice(None), pl.ds(start, min(piece, positions - start)))
        copies.append(pltpu.make_async_copy(cache_hbm.at[at], held.at[at], sems.at[k + 2]))
        copies[-1].start()
    first.wait()
    second.wait()
    factor = (HD + ROPE) ** (-0.5)
    queries = queries_ref[...].T
    new = new_ref[...].astype(F32)
    own = jnp.sum(queries.astype(F32) * new, axis=1, keepdims=True) * factor
    scores, highest = [], own
    for k, start in enumerate(range(0, positions, piece)):
        size = min(piece, positions - start)
        copies[k].wait()
        part = jnp.dot(queries, held[:, start : start + size], preferred_element_type=F32)
        place = lax.broadcasted_iota(jnp.int32, (1, size), 1) + start
        part = jnp.where(place < length_ref[0], part * factor, -jnp.inf)
        scores.append(part)
        highest = jnp.maximum(highest, jnp.max(part, axis=1, keepdims=True))
    total = jnp.exp(own - highest)
    expos = [jnp.exp(part - highest) for part in scores]
    for expo in expos:
        total = total + jnp.sum(expo, axis=1, keepdims=True)
    share = 1.0 / total
    own = (jnp.exp(own - highest) * share).astype(BF).astype(F32)
    probs = jnp.concatenate([(expo * share).astype(BF) for expo in expos], axis=1)
    latent = lax.dot_general(held[:LAT, :], probs, NT, preferred_element_type=F32)
    latent = latent.T + own * new[:, :LAT]
    count, heads = out_ref.shape[0] // 2, out_ref.shape[1]
    latent = latent.reshape(count, heads, LAT).astype(BF)
    out_ref[:count] = latent
    out_ref[count:] = latent


def exchange(array, axis, groups):
    return lax.all_to_all(
        array, axis, split_axis=0, concat_axis=0, axis_index_groups=groups, tiled=True
    )


def sum_scatter(terms, axis, count, groups=None):
    return add_blocks(exchange(terms, axis, groups), count)


def add_blocks(got, count):
    got = got.reshape((count, got.shape[0] // count) + got.shape[1:])
    return jnp.sum(got.astype(F32), axis=0)


def gather_rows(rows, axis, count, groups=None):
    copies = jnp.broadcast_to(rows[None], (count,) + rows.shape)
    got = exchange(copies, axis, groups)
    return got.reshape((count * rows.shape[0],) + rows.shape[1:])


def local(
    queries,
    latent_cache,
    new_latent,
    lengths,
    order,
    value_up,
    out_proj,
    residual,
    norm_gain,
    gate_weight,
    up_weight,
    down_weight,
    n_dp,
    n_tp,
):
    core = lax.rem(lax.axis_index("dp"), 2)
    swap = [(i, i ^ 1) for i in range(n_dp)]
    n_x = n_dp // 4
    tp = lax.axis_index("tp")

    def at(y, x, c):
        return (y * n_x + x) * 2 + c

    xs, two = range(n_x), range(2)
    along_x = [[at(y, x, c) for x in xs] for y in two for c in two]
    same_y = [[at(y, x, c) for x in xs for c in two] for y in two]
    across_y = [(i, (i + n_dp // 2) % n_dp) for i in range(n_dp)]
    out_proj2 = lax.ppermute(out_proj, "dp", swap)
    norm_gain2 = lax.ppermute(norm_gain, "dp", swap)
    positions = latent_cache.shape[1]
    copies = pl.pallas_call(
        attend_kernel,
        out_shape=jax.ShapeDtypeStruct((2 * n_tp, queries.shape[1] // n_tp, LAT), BF),
        in_specs=[SMEM] + [pl.BlockSpec(memory_space=pltpu.HBM)] * 3,
        out_specs=VMEM,
        scratch_shapes=[
            pltpu.VMEM((LAT + ROPE, positions), BF),
            pltpu.VMEM((LAT + ROPE, queries.shape[1]), BF),
            pltpu.VMEM((1, LAT + ROPE), BF),
            pltpu.SemaphoreType.DMA(((positions + 511) // 512 + 2,)),
        ],
        compiler_params=pltpu.CompilerParams(vmem_limit_bytes=63 * 2**20 + 15 * 2**16),
    )(lengths, queries[0].T, new_latent, latent_cache[0].T)
    both_y = [
        [at(y, x, c) * n_tp + j for y in two for j in range(n_tp)] for x in xs for c in two
    ]
    heads, _, size = value_up.shape
    copies, value_up, residual = lax.optimization_barrier((copies, value_up, residual))
    owned = exchange(copies, ("dp", "tp"), both_y)
    maps = value_up.transpose(1, 0, 2).reshape(LAT, heads * size)
    residual2 = lax.ppermute(residual, "dp", swap)
    owned, maps, residual2 = lax.optimization_barrier((owned, maps, residual2))
    copies = call(
        value_kernel,
        jax.ShapeDtypeStruct((n_x, owned.shape[0], heads * size), BF),
        [VMEM] * 2,
        2 * owned.size * heads * size,
    )(owned, maps)
    heads_set = exchange(copies, "dp", along_x).reshape(-1, heads * size)
    places = jnp.arange(n_dp // 2 * n_tp)
    set_dp = (places // n_tp % 2 * n_x + places // (2 * n_tp)) * 2
    set_rows = set_dp * n_tp + places % n_tp
    count = residual.shape[0]
    res_row = tp * count
    res_dp = lax.div(res_row, n_tp)
    res_x, res_y = lax.rem(lax.div(res_dp, 2), n_x), lax.div(res_dp, 2 * n_x)
    first = (res_x * 2 + res_y) * n_tp + lax.rem(res_row, n_tp)
    first = jnp.where(lax.rem(res_dp, 2) == core, first, -count).reshape(1)
    res_pair = jnp.concatenate([residual, residual2], axis=1)
    attn_terms = call(
        attn_kernel,
        jax.ShapeDtypeStruct((heads_set.shape[0], res_pair.shape[1]), BF),
        [SMEM] + [VMEM] * 4,
        2 * heads_set.size * res_pair.shape[1],
    )(first, heads_set, out_proj.T, out_proj2.T, res_pair)
    width = residual.shape[1]
    attn_terms, gate_weight, up_weight = lax.optimization_barrier(
        (attn_terms, gate_weight, up_weight)
    )
    got = exchange(attn_terms, "tp", None)
    gate_weight2 = lax.ppermute(gate_weight, "dp", swap)
    up_weight2 = lax.ppermute(up_weight, "dp", swap)
    got, gate_weight2, up_weight2 = lax.optimization_barrier((got, gate_weight2, up_weight2))
    got = got.reshape(n_tp, -1, got.shape[1])
    copies = call(mid_kernel, jax.ShapeDtypeStruct(got.shape, BF), [VMEM], got.size)(got)
    mid_set = exchange(copies, "tp", None).reshape(-1, got.shape[2])
    mid_here, mid_there = mid_set[:, :width], mid_set[:, width:]
    gain = jnp.concatenate([norm_gain, norm_gain2])[None, :]
    ff = gate_weight.shape[1]
    tall = mid_set.shape[0] // n_x * (2 * ff // LANES) + 16
    terms = call(
        ff_kernel,
        jax.ShapeDtypeStruct((n_x, tall, LANES), BF),
        [VMEM] * 6,
        4 * mid_set.size * ff,
    )(mid_set, gain, gate_weight, gate_weight2, up_weight, up_weight2)
    got = exchange(terms, "dp", along_x).reshape(-1, LANES)
    sums = add_blocks(got, n_x)
    theirs = lax.ppermute(sums.astype(BF), "dp", across_y)
    copies = call(
        hidden_kernel,
        jax.ShapeDtypeStruct((n_x * 2, 2 * n_tp * ff // LANES, LANES), BF),
        [VMEM] * 2,
        8 * sums.size,
    )(sums, theirs)
    copies, order, mid_there = lax.optimization_barrier((copies, order, mid_there))
    mid_rest = lax.ppermute(mid_there, "dp", swap)
    hidden = exchange(copies, "dp", same_y)
    rows = n_dp * n_tp
    spots = jnp.arange(rows)
    spot_dp = at(spots // n_tp % 2, spots // (4 * n_tp), spots // (2 * n_tp) % 2)
    spot_rows = spot_dp * n_tp + spots % n_tp
    own_count = rows // n_tp
    listed = order.reshape(n_tp, 2, own_count // 2).swapaxes(0, 1).reshape(rows)
    pick = (listed[:, None] == spot_rows[None, :]).astype(BF)
    hidden, pick, mid_rest = lax.optimization_barrier((hidden, pick, mid_rest))
    width = down_weight.shape[1]
    ffn_terms = call(
        down_kernel,
        jax.ShapeDtypeStruct((rows // 2, 2 * width), BF),
        [VMEM] * 3,
        2 * rows * ff * (rows + width),
    )(pick, hidden, down_weight.T)
    wanted = lax.dynamic_slice_in_dim(order, tp * own_count, own_count)
    pick1 = (wanted[:, None] == (set_rows + core * n_tp)[None, :]).astype(BF)
    pick2 = (wanted[:, None] == (set_rows + (1 - core) * n_tp)[None, :]).astype(BF)
    mid_rows = jnp.dot(pick1, mid_here, preferred_element_type=F32) + jnp.dot(
        pick2, mid_rest, preferred_element_type=F32
    )
    got = exchange(ffn_terms, "tp", None)
    got, mid_rows = lax.optimization_barrier((got, mid_rows))
    ffn_own = add_blocks(got, n_tp)
    ffn_own = jnp.concatenate([ffn_own[:, :width], ffn_own[:, width:]], axis=0)
    return (mid_rows + ffn_own).astype(BF)


def solution(mesh):
    n_dp, n_tp = mesh.shape["dp"], mesh.shape["tp"]

    def run(*args):
        return local(*args, n_dp=n_dp, n_tp=n_tp)

    placed = (
        P(("dp", "tp"), None, None),
        P(("dp", "tp"), None, None),
        P(("dp", "tp"), None),
        P(("dp", "tp")),
        P(),
        P("tp", None, None),
        P("tp", "dp"),
        P("tp", "dp"),
        P("dp"),
        P("dp", "tp"),
        P("dp", "tp"),
        P("tp", "dp"),
    )
    return jax.shard_map(
        run, mesh=mesh, in_specs=placed, out_specs=P("tp", "dp"), check_vma=False
    )
```
